512 devices in a mesh: lon: 16 (over x_lo, z), lat: 16 (over y, core), dp: 2 (over x_hi).
Axes of the slice: x: 4 (x_hi: 2, x_lo: 2; x = x_hi * 2 + x_lo), y: 8, z: 8, core: 2. Of those that a mesh axis runs over, the one named last changes fastest.
Arguments:
- output_first: bfloat16 [2, 4, 96, 192, 192], P('dp', None, 'lat', 'lon'), may hold values from -6 to 6
- output_second: bfloat16 [2, 4, 96, 192, 192], P('dp', None, 'lat', 'lon')
- cotangent_first: bfloat16 [2, 4, 96, 192, 192], P('dp', None, 'lat', 'lon'), may hold values from -6 to 6
- cotangent_second: bfloat16 [2, 4, 96, 192, 192], P('dp', None, 'lat', 'lon'), may hold values from -6 to 6
- norm_gain: float32 [192], replicated, may hold values from 0.5 to 1.5
- w_qkv: bfloat16 [192, 576], replicated, may hold values from -0.4375 to 0.4375
- w_proj: bfloat16 [192, 192], replicated, may hold values from -0.4375 to 0.4375
- earth_bias: float32 [2, 16, 6, 3312], P(None, 'lat'), may hold values from -4 to 300
- shifts: int32 [2], replicated, may hold values from 1 to 6, as said below
- region: int32 [96, 192], replicated, may hold values from 0 to 1, as said below
Outputs:
- input_first: bfloat16 [2, 4, 96, 192, 192], P('dp', None, 'lat', 'lon')
- grad_second: bfloat16 [2, 4, 96, 192, 192], P('dp', None, 'lat', 'lon')
- bias_grad: float32 [2, 16, 6, 3312], P(None, 'lat')
The draws below stay inside these ranges and needn't reach their ends.
Inputs may be any that keep to these rules, and one draw needn't show every extreme that they name: shifts[0] is the latitude offset, from 1 to 5; shifts[1] is the longitude offset and equals 6. region is 1 on the framed rows r >= 96 - shifts[0], whose cells came round from the other edge of the latitude range, and 0 on all other rows; it does not vary with longitude.
All inputs are finite; a program needn't handle non-finite values.
Results may differ from the reference program's by a relative error of at most 0.012.
Values may be sent and summed in bfloat16 or wider, within the bound.
No kernel may reach another device: no remote copies, remote signals or barrier semaphores. Data moves between devices by JAX's collectives and lax.ppermute only.
A program may use at most 128 MiB of HBM per device.

```python
import math
import jax
import jax.numpy as jnp
from jax import lax

C = 192
HEADS = 6
LEVELS = 4
WZ = 2
WL = 6
WC = 12
WT = 144
POS = 3312
SAMPLES = 2
LAT = 96
LON = 192
ZT = 2
LATW = 16


def lat_offset(key):
    return jax.random.randint(key, (1,), 1, WL).astype(jnp.int32)


def draw_output_second(key, part):
    key = jax.random.fold_in(key, 11)
    keys = jax.random.split(key, 3)
    shape_full = (SAMPLES, LEVELS, LAT, LON, C)
    row_scale = jnp.exp(jax.random.uniform(keys[1], (SAMPLES, LEVELS, LAT, LON, 1), jnp.float32, 0.0, math.log(10.0)))
    col_scale = jnp.exp(jax.random.uniform(keys[2], (C,), jnp.float32, 0.0, math.log(10.0)))
    values = jax.random.normal(keys[0], shape_full, jnp.float32) * col_scale * row_scale * 0.3
    return values.astype(jnp.bfloat16)


def draw_earth_bias(key, part):
    key = jax.random.fold_in(key, 23)
    keys = jax.random.split(key, 1)
    shape_full = (ZT, LATW, HEADS, POS)
    values = jnp.clip(jax.random.normal(keys[0], shape_full, jnp.float32), -4.0, 4.0)
    return values.astype(jnp.float32)


def draw_shifts(key, part):
    lat_part = lat_offset(key)
    lon_part = jnp.full((1,), WC // 2, jnp.int32)
    return jnp.concatenate((lat_part, lon_part)).astype(jnp.int32)


def draw_region(key, part):
    lat_part = lat_offset(key)
    rows = jnp.arange(LAT, dtype=jnp.int32)
    band = (rows >= LAT - lat_part[0]).astype(jnp.int32)
    return jnp.broadcast_to(band[:, None], (LAT, LON)).astype(jnp.int32)


def level_of(stream_key, shape, cuts, smallest, high):
    factor_of, own = 1.0, jax.random.fold_in(stream_key, 6)
    for dim, shards_of in cuts:
        draws = jnp.exp(jax.random.uniform(jax.random.fold_in(own, dim), (shards_of,), jnp.float32, smallest / len(cuts), high / len(cuts)))
        factor_of = factor_of * jnp.repeat(draws, shape[dim] // shards_of).reshape([-1 if axis == dim else 1 for axis in range(len(shape))])
    return factor_of


def bell_draw(rng, dims, width, reach, shards=(), kind=jnp.bfloat16):
    factor_of = level_of(rng, dims, shards, -0.22, 0.18) if shards else 1.0
    drawn = jax.random.normal(rng, dims, jnp.float32) * width * factor_of
    return jnp.minimum(jnp.maximum(drawn, -reach), reach).astype(kind)


def setup_inputs(seed: int = 0) -> dict:
    splits = jax.random.split(jax.random.key(seed), 11)
    return {
        "output_first": bell_draw(splits[0], (SAMPLES, LEVELS, LAT, LON, C), 1.0, 6.0, ((0, 2), (2, 16), (3, 16))),
        "output_second": draw_output_second(jax.random.fold_in(splits[10], 71), 0),
        "cotangent_first": bell_draw(splits[2], (SAMPLES, LEVELS, LAT, LON, C), 1.0, 6.0, ((0, 2), (2, 16), (3, 16))),
        "cotangent_second": bell_draw(splits[3], (SAMPLES, LEVELS, LAT, LON, C), 1.0, 6.0, ((0, 2), (2, 16), (3, 16))),
        "norm_gain": jnp.clip(1.0 + 0.1 * jax.random.normal(splits[4], (C,), jnp.float32), 0.5, 1.5),
        "w_qkv": bell_draw(splits[5], (C, 3 * C), C ** -0.5, 0.4375),
        "w_proj": bell_draw(splits[6], (C, C), C ** -0.5, 0.4375),
        "earth_bias": draw_earth_bias(jax.random.fold_in(splits[10], 71), 0),
        "shifts": draw_shifts(jax.random.fold_in(splits[10], 71), 0),
        "region": draw_region(jax.random.fold_in(splits[10], 71), 0),
    }


norm_eps = 1e-05
mask_fill = -1e+30

def layer_norm(values):
    as_float = values.astype(jnp.float32)
    centered = as_float - lax.optimization_barrier(jnp.mean(as_float, axis=-1, keepdims=True))
    inverse = lax.rsqrt(lax.optimization_barrier(jnp.mean(centered * centered, axis=-1, keepdims=True)) + norm_eps)
    return (centered * inverse, inverse)

def norm_backward(normed, inverse, norm_gain, upstream):
    scaled = upstream * norm_gain
    return inverse * (scaled - lax.optimization_barrier(jnp.mean(scaled, axis=-1, keepdims=True)) - normed * lax.optimization_barrier(jnp.mean(scaled * normed, axis=-1, keepdims=True)))

def offset_table(span_width):
    starts = jnp.arange(span_width)[:, None]
    finish = jnp.arange(span_width)[None, :]
    offsets = (finish - starts + span_width - 1).reshape(span_width * span_width)
    return (offsets[:, None] == jnp.arange(2 * span_width - 1)[None, :]).astype(jnp.float32)

def expand_bias(bias_table):
    leading = bias_table.shape[:-1]
    ndim_lead = len(leading)
    combos = bias_table.reshape(leading + (WZ * WZ * WL * WL, 2 * WC - 1))
    spread = jnp.einsum('...pd,qd->...pq', combos, offset_table(WC), precision=lax.Precision.HIGHEST)
    spread = spread.reshape(leading + (WZ, WZ, WL, WL, WC, WC))
    axis_order = tuple(range(ndim_lead)) + tuple((ndim_lead + position for position in (0, 2, 4, 1, 3, 5)))
    return spread.transpose(axis_order).reshape(leading + (WT, WT))

def compress_bias(score_grad):
    leading = score_grad.shape[:-2]
    ndim_lead = len(leading)
    unpacked = score_grad.reshape(leading + (WZ, WL, WC, WZ, WL, WC))
    axis_order = tuple(range(ndim_lead)) + tuple((ndim_lead + position for position in (0, 3, 1, 4, 2, 5)))
    paired = unpacked.transpose(axis_order).reshape(leading + (WZ * WZ * WL * WL, WC * WC))
    folded = jnp.einsum('...pq,qd->...pd', paired, offset_table(WC), precision=lax.Precision.HIGHEST)
    return folded.reshape(leading + (POS,))

def to_groups(volume):
    samples, levels, lat_size, lon_size, features = volume.shape
    unpacked = volume.reshape(samples, levels // WZ, WZ, lat_size // WL, WL, lon_size // WC, WC, features)
    grouped = unpacked.transpose(0, 3, 1, 5, 2, 4, 6, 7)
    return grouped.reshape(samples * (lat_size // WL), levels // WZ * (lon_size // WC), WT, features)

def from_groups(grouped, shape_out):
    samples, levels, lat_size, lon_size, features = shape_out
    unpacked = grouped.reshape(samples, lat_size // WL, levels // WZ, lon_size // WC, WZ, WL, WC, features)
    return unpacked.transpose(0, 2, 4, 1, 5, 3, 6, 7).reshape(shape_out)

def region_windows(id_block):
    lat_size, lon_size = id_block.shape
    unpacked = id_block.reshape(lat_size // WL, WL, lon_size // WC, WC).transpose(0, 2, 1, 3)
    spread = jnp.broadcast_to(unpacked[:, :, None], (lat_size // WL, lon_size // WC, WZ, WL, WC))
    return spread.reshape(lat_size // WL, lon_size // WC, WT)

def attend(win_input, win_upstream, w_qkv, bias_full, allowed):
    win_count = win_input.shape[0]
    head_dim = win_input.shape[2] // HEADS
    score_scale = head_dim ** (-0.5)
    packed = jnp.einsum('ntc,cf->ntf', win_input.astype(jnp.float32), w_qkv.astype(jnp.float32)).astype(jnp.bfloat16)
    packed = packed.reshape(win_count, WT, 3, HEADS, head_dim).astype(jnp.float32)
    queries = packed[:, :, 0]
    key_rows = packed[:, :, 1]
    value_rows = packed[:, :, 2]
    scores = jnp.einsum('nihd,njhd->nhij', queries, key_rows) * score_scale + bias_full
    scores = jnp.where(allowed[:, None], scores, mask_fill)
    largest = lax.optimization_barrier(jnp.max(scores, axis=-1, keepdims=True))
    exponent = jnp.exp(scores - largest)
    weights = exponent / lax.optimization_barrier(jnp.sum(exponent, axis=-1, keepdims=True))
    weights_low = weights.astype(jnp.bfloat16).astype(jnp.float32)
    attended = jnp.einsum('nhij,njhd->nihd', weights_low, value_rows).astype(jnp.bfloat16)
    attended_wide = attended.astype(jnp.float32)
    upstream = win_upstream.reshape(win_count, WT, HEADS, head_dim).astype(jnp.float32)
    grad_weights = jnp.einsum('nihd,njhd->nhij', upstream, value_rows)
    row_dot = jnp.einsum('nihd,nihd->nhi', upstream, attended_wide)
    grad_scores = weights * (grad_weights - row_dot[..., None])
    grad_low = grad_scores.astype(jnp.bfloat16).astype(jnp.float32)
    grad_query = jnp.einsum('nhij,njhd->nihd', grad_low, key_rows) * score_scale
    grad_key = jnp.einsum('nhij,nihd->njhd', grad_low, queries) * score_scale
    grad_value = jnp.einsum('nhij,nihd->njhd', weights_low, upstream)
    coeffs = jnp.stack((grad_query, grad_key, grad_value), axis=2).astype(jnp.bfloat16)
    coeffs = coeffs.reshape(win_count, WT, 3 * HEADS * head_dim)
    return (attended.reshape(win_count, WT, HEADS * head_dim), coeffs, grad_scores)

def reference(output_first, output_second, cotangent_first, cotangent_second, norm_gain, w_qkv, w_proj, earth_bias, shifts, region):
    samples = output_first.shape[0]
    normed, inverse = layer_norm(output_second)
    hidden = (normed * norm_gain).astype(jnp.bfloat16)
    upstream = jnp.dot(cotangent_first.reshape(-1, C), w_proj.T, preferred_element_type=jnp.float32)
    upstream = upstream.astype(jnp.bfloat16).reshape(hidden.shape)
    lat_shift = shifts[0]
    lon_shift = shifts[1]
    framed_hidden = jnp.roll(hidden, (-lat_shift, -lon_shift), axis=(2, 3))
    framed_up = jnp.roll(upstream, (-lat_shift, -lon_shift), axis=(2, 3))
    group_hidden = to_groups(framed_hidden)
    group_up = to_groups(framed_up)
    region_ids = region_windows(region)
    allowed_all = region_ids[..., :, None] == region_ids[..., None, :]
    bias_all = expand_bias(earth_bias)
    lon_count = LON // WC

    def one_group(group_index):
        lat_band = group_index % LATW
        bias_group = jnp.broadcast_to(bias_all[:, lat_band][:, None], (ZT, lon_count, HEADS, WT, WT))
        bias_group = bias_group.reshape(ZT * lon_count, HEADS, WT, WT)
        allowed_group = jnp.broadcast_to(allowed_all[lat_band][None], (ZT, lon_count, WT, WT)).reshape(-1, WT, WT)
        attended, coeffs, grad_scores = attend(group_hidden[group_index], group_up[group_index], w_qkv, bias_group, allowed_group)
        feature_grad = jnp.dot(coeffs.reshape(-1, 3 * C), w_qkv.T, preferred_element_type=jnp.float32).astype(jnp.bfloat16)
        bias_part = grad_scores.reshape(ZT, lon_count, HEADS, WT, WT).sum(axis=1)
        return (attended, feature_grad.reshape(-1, WT, C), bias_part)
    attended, feature_grad, bias_parts = lax.map(one_group, jnp.arange(samples * LATW))
    attended_home = jnp.roll(from_groups(attended, hidden.shape), (lat_shift, lon_shift), axis=(2, 3))
    mixed_out = jnp.dot(attended_home.reshape(-1, C), w_proj, preferred_element_type=jnp.float32).reshape(hidden.shape)
    input_first = (output_first.astype(jnp.float32) - mixed_out).astype(jnp.bfloat16)
    grad_home = jnp.roll(from_groups(feature_grad, hidden.shape), (lat_shift, lon_shift), axis=(2, 3))
    grad_home = lax.optimization_barrier(grad_home).astype(jnp.float32)
    grad_second = (cotangent_second.astype(jnp.float32) + norm_backward(normed, inverse, norm_gain, grad_home)).astype(jnp.bfloat16)
    bias_sum = bias_parts.reshape(samples, LATW, ZT, HEADS, WT, WT).sum(axis=0).transpose(1, 0, 2, 3, 4)
    bias_grad = compress_bias(bias_sum)
    return (input_first, grad_second, bias_grad)
```

```python
import functools

import jax
import jax.numpy as jnp
from jax import lax
from jax.experimental import pallas as pl
from jax.experimental.pallas import tpu as pltpu
from jax.sharding import PartitionSpec as P

C = 192
HEADS = 6
HEAD = 32
LEVELS = 4
WL = 6
WC = 12
HALF = 6
POS = 3312
CHUNK = 138
SPAN = 23
GROUPS = 12
ROWS = 192
LANES = 384
CELLS = 288
PITCH = 16
WIDE = 3584
FOLD = 1664

norm_eps = 1e-05
mask_fill = -1e30
scale = HEAD**-0.5
vmem_bytes = 40 * 1024 * 1024

f32 = jnp.float32
bf16 = jnp.bfloat16


def iota(shape, dim):
    return lax.broadcasted_iota(jnp.int32, shape, dim)


def mm(a, b):
    return lax.dot_general(a, b, (((1,), (0,)), ((), ())), preferred_element_type=f32)


def mm_t(a, b):
    return lax.dot_general(a, b, (((1,), (1,)), ((), ())), preferred_element_type=f32)


def parts(index, size):
    return lax.div(index, jnp.int32(size)), lax.rem(index, jnp.int32(size))


def picks(index, count, dim):
    shape = (index.shape[0], count) if dim == 0 else (count, index.shape[1])
    return jnp.where(iota(shape, 1 - dim) == index, 1.0, 0.0).astype(bf16)


def line(size, dim):
    return iota((size, 1) if dim == 0 else (1, size), dim)


def query_cells(a, dim):
    column, group = parts(line(ROWS, dim), PITCH)
    level, row = parts(group, WL)
    return jnp.where(group < GROUPS, (row * WC + column) * LEVELS + 2 * a + level, -1)


def key_cells(a, dim):
    group, column = parts(line(LANES, dim), 32)
    level, row = parts(group, WL)
    return jnp.where(column < WC, (row * WC + column) * LEVELS + 2 * a + level, -1)


def spread_matrix(level, dim):
    group, place = parts(line(LANES, dim), 32)
    group = group - level * WL
    entry = jnp.where(
        (group >= 0) & (group < WL) & (place < SPAN), group * SPAN + place, -1
    )
    return picks(entry, LANES, dim)


def chunk_place(group, level):
    start = (((group // WL) * 2 + level) * WL + group % WL) * CHUNK
    return start // 128 * 128, start % 128


def table_kernel(bias_ref, table_ref, wide, pieces):
    wide[...] = jnp.zeros(wide.shape, f32)
    for a in range(2):
        for h in range(HEADS):
            wide[a * 8 + h : a * 8 + h + 1, 0:POS] = bias_ref[a * HEADS + h]
    total = jnp.zeros((ROWS, LANES), f32)
    for level in range(2):
        for group in range(GROUPS):
            tile, shift = chunk_place(group, level)
            piece = wide[:, tile : tile + LANES]
            if shift:
                piece = pltpu.roll(piece, LANES - shift, 1)
            pieces[group * PITCH : (group + 1) * PITCH, :] = piece
        spread = spread_matrix(level, 1)
        rest = pieces[...]
        for _ in range(3):
            part = rest.astype(bf16)
            total = total + mm(part, spread)
            rest = rest - part.astype(f32)
    pieces[...] = total
    table_ref[...] = jnp.zeros(table_ref.shape, f32)
    for group in range(GROUPS):
        for place in range(16):
            row = group * PITCH + place
            table_ref[place, group : group + 1, :] = pieces[row : row + 1, :]


def main_kernel(
    meta_ref,
    own_ref,
    east_ref,
    south_ref,
    diag_ref,
    gain_ref,
    w_qkv_ref,
    w_qkv_t_ref,
    w_proj_ref,
    table_ref,
    own_out,
    east_out,
    bias_out,
    framed,
    mask,
    queries,
    ups,
    queries_t,
    ups_t,
    keys_t,
    values_t,
    attended_t,
    grad_query_t,
    grad_key_t,
    grad_value_t,
    table_grad,
    wide,
    folds,
):
    shift = meta_ref[0]
    edge = meta_ref[1]

    half = HALF * LEVELS
    for r in range(WL):
        place = r + shift
        inside = place < WL
        near = jnp.minimum(place, WL - 1)
        far = jnp.maximum(place - WL, 0)
        left = jnp.where(inside, own_ref[near].astype(f32), south_ref[far].astype(f32))
        right = jnp.where(inside, east_ref[near].astype(f32), diag_ref[far].astype(f32))
        framed[2 * r * half : (2 * r + 1) * half, :] = left.reshape(half, 2 * C)
        framed[(2 * r + 1) * half : (2 * r + 2) * half, :] = right.reshape(half, 2 * C)

    cells = framed[:, 0:C]
    cotangent = framed[:, C : 2 * C].astype(bf16)
    centered = cells - jnp.mean(cells, axis=-1, keepdims=True)
    inverse = lax.rsqrt(jnp.mean(centered * centered, axis=-1, keepdims=True) + norm_eps)
    hidden = (centered * inverse * gain_ref[...]).astype(bf16)

    w_proj = w_proj_ref[...]
    for a in range(2):
        to_queries = picks(query_cells(a, 0), CELLS, 0)
        turned = mm(to_queries, hidden).astype(bf16)
        turned_cot = mm(to_queries, cotangent).astype(bf16)
        spaced = mm(picks(key_cells(a, 0), CELLS, 0), hidden).astype(bf16)
        queries[a] = mm(turned, w_qkv_ref[:, 0:C]).astype(bf16)
        queries_t[a] = mm_t(w_qkv_t_ref[0:C, :], turned).astype(bf16)
        keys_t[a] = mm_t(w_qkv_t_ref[C : 2 * C, :], spaced).astype(bf16)
        values_t[a] = mm_t(w_qkv_t_ref[2 * C : 3 * C, :], spaced).astype(bf16)
        ups[a] = mm_t(turned_cot, w_proj).astype(bf16)
        ups_t[a] = mm_t(w_proj, turned_cot).astype(bf16)

    query_row = parts(parts(line(ROWS, 0), PITCH)[1], WL)[1]
    key_group, key_column = parts(line(LANES, 1), 32)
    key_row = parts(key_group, WL)[1]
    query_id = jnp.where(query_row >= edge, 1, 0)
    key_id = jnp.where(key_column < WC, jnp.where(key_row >= edge, 1, 0), 2)
    mask[...] = jnp.where(query_id == key_id, 0.0, mask_fill)
    table_grad[...] = jnp.zeros(table_grad.shape, f32)

    def one_head(h, carry):
        features = pl.ds(pl.multiple_of(h * HEAD, HEAD), HEAD)
        chosen = iota((1, C), 1) // HEAD == h
        for a in range(2):
            query = jnp.where(chosen, queries[a], jnp.zeros((), bf16))
            up = jnp.where(chosen, ups[a], jnp.zeros((), bf16))
            scores = mm(query, keys_t[a]) * scale
            table = table_ref[a * 8 + h]
            bias = jnp.concatenate(
                [
                    pltpu.roll(table, (c - WC + 1) % LANES, 1) if c != WC - 1 else table
                    for c in range(WC)
                ],
                axis=0,
            )
            scores = scores + bias + mask[...]
            exponent = jnp.exp(scores - jnp.max(scores, axis=-1, keepdims=True))
            weights = exponent * (1.0 / jnp.sum(exponent, axis=-1, keepdims=True))
            weights_low = weights.astype(bf16)
            grad_weights = mm(up, values_t[a])
            row_dot = jnp.sum(weights * grad_weights, axis=-1, keepdims=True)
            grad_scores = weights * (grad_weights - row_dot)
            grad_low = grad_scores.astype(bf16)
            attended_t[a, features, :] = mm_t(values_t[a, features, :], weights_low).astype(bf16)
            grad_value_t[a, features, :] = mm(ups_t[a, features, :], weights_low).astype(bf16)
            grad_query_t[a, features, :] = (
                mm_t(keys_t[a, features, :], grad_low) * scale
            ).astype(bf16)
            grad_key_t[a, features, :] = (
                mm(queries_t[a, features, :], grad_low) * scale
            ).astype(bf16)
            folded = grad_scores[(WC - 1) * PITCH : WC * PITCH]
            for c in range(WC - 1):
                folded = folded + pltpu.roll(
                    grad_scores[c * PITCH : (c + 1) * PITCH], WC - 1 - c, 1
                )
            table_grad[a * 8 + h] = folded
        return carry

    lax.fori_loop(0, HEADS, one_head, 0)

    group, place = parts(line(ROWS, 0), PITCH)
    by_group = mm(
        picks(place * PITCH + group, 256, 0),
        table_grad[...].reshape(256, LANES).astype(bf16),
    ).astype(bf16)
    wide[...] = jnp.zeros(wide.shape, f32)
    for level in range(2):
        packed = mm(by_group, spread_matrix(level, 0))
        for group in range(GROUPS):
            tile, turn = chunk_place(group, level)
            piece = packed[group * PITCH : (group + 1) * PITCH]
            if turn:
                piece = pltpu.roll(piece, turn, 1)
            wide[:, tile : tile + LANES] += piece
    for side in range(2):
        for a in range(2):
            start = (2 * side + a) * HEADS
            folds[start : start + HEADS, :] = wide[
                a * 8 : a * 8 + HEADS, side * FOLD : (side + 1) * FOLD
            ]
    bias_out[...] = folds[...].astype(bf16)

    attended = jnp.zeros((CELLS, C), f32)
    coeffs = [jnp.zeros((CELLS, C), f32) for _ in range(3)]
    for a in range(2):
        from_queries = picks(query_cells(a, 1), CELLS, 1)
        from_keys = picks(key_cells(a, 1), CELLS, 1)
        attended = attended + mm_t(from_queries, attended_t[a])
        coeffs[0] = coeffs[0] + mm_t(from_queries, grad_query_t[a])
        coeffs[1] = coeffs[1] + mm_t(from_keys, grad_key_t[a])
        coeffs[2] = coeffs[2] + mm_t(from_keys, grad_value_t[a])
    framed[:, 0:C] = attended
    framed[:, C : 2 * C] = sum(
        mm(coeffs[part].astype(bf16), w_qkv_t_ref[part * C : (part + 1) * C, :])
        for part in range(3)
    )
    for r in range(WL):
        left = framed[2 * r * half : (2 * r + 1) * half, :]
        right = framed[(2 * r + 1) * half : (2 * r + 2) * half, :]
        own_out[r] = left.reshape(HALF, LEVELS, 2 * C).astype(bf16)
        east_out[r] = right.reshape(HALF, LEVELS, 2 * C).astype(bf16)


def home_kernel(
    meta_ref,
    own_ref,
    west_ref,
    north_ref,
    corner_ref,
    output_first_ref,
    output_second_ref,
    cotangent_second_ref,
    gain_ref,
    w_proj_ref,
    input_first_out,
    grad_second_out,
    placed,
):
    shift = meta_ref[0]
    half = HALF * LEVELS
    for r in range(WL):
        place = r - shift
        inside = place >= 0
        near = jnp.maximum(place, 0)
        far = jnp.minimum(place + WL, WL - 1)
        left = jnp.where(inside, west_ref[near].astype(f32), corner_ref[far].astype(f32))
        right = jnp.where(inside, own_ref[near].astype(f32), north_ref[far].astype(f32))
        placed[2 * r * half : (2 * r + 1) * half, :] = left.reshape(half, 2 * C)
        placed[(2 * r + 1) * half : (2 * r + 2) * half, :] = right.reshape(half, 2 * C)
    shape = (WL, WC, LEVELS, C)
    mixed = mm(placed[:, 0:C].astype(bf16), w_proj_ref[...])
    first = output_first_ref[...].astype(f32).reshape(CELLS, C)
    input_first_out[...] = (first - mixed).reshape(shape).astype(bf16)

    cells = output_second_ref[...].astype(f32).reshape(CELLS, C)
    centered = cells - jnp.mean(cells, axis=-1, keepdims=True)
    inverse = lax.rsqrt(jnp.mean(centered * centered, axis=-1, keepdims=True) + norm_eps)
    normed = centered * inverse
    scaled = placed[:, C : 2 * C] * gain_ref[...]
    backward = inverse * (
        scaled
        - jnp.mean(scaled, axis=-1, keepdims=True)
        - normed * jnp.mean(scaled * normed, axis=-1, keepdims=True)
    )
    second = cotangent_second_ref[...].astype(f32).reshape(CELLS, C)
    grad_second_out[...] = (second + backward).reshape(shape).astype(bf16)


def table_home_kernel(mine_ref, other_ref, table_out):
    total = mine_ref[...].astype(f32) + other_ref[...].astype(f32)
    rows = 2 * HEADS
    for row in range(rows):
        table_out[row, :, 0:FOLD] = total[row : row + 1]
        table_out[row, :, FOLD:POS] = total[rows + row : rows + row + 1, 0 : POS - FOLD]


def vmem(count):
    return [pl.BlockSpec(memory_space=pltpu.VMEM)] * count


def smem():
    return [pl.BlockSpec(memory_space=pltpu.SMEM)]


params = pltpu.CompilerParams(vmem_limit_bytes=vmem_bytes)


def cost(flops, moved):
    return pl.CostEstimate(flops=flops, bytes_accessed=moved, transcendentals=0)


def shifted(x, lat_step, lon_step):
    lats, lons = lax.axis_size("lat"), lax.axis_size("lon")
    if not lat_step:
        return lax.ppermute(x, "lon", [(i, (i + lon_step) % lons) for i in range(lons)])
    if not lon_step:
        return lax.ppermute(x, "lat", [(i, (i + lat_step) % lats) for i in range(lats)])
    pairs = [
        (j * lats + i, (j + lon_step) % lons * lats + (i + lat_step) % lats)
        for j in range(lons)
        for i in range(lats)
    ]
    return lax.ppermute(x, ("lon", "lat"), pairs)


def partner(x, axis, stride):
    return lax.ppermute(x, axis, [(i, i ^ stride) for i in range(lax.axis_size(axis))])


def by_cell(x):
    return x[0].transpose(1, 2, 0, 3)


def local(
    output_first,
    output_second,
    cotangent_first,
    cotangent_second,
    norm_gain,
    w_qkv,
    w_proj,
    earth_bias,
    shifts,
    region,
):
    second_cells = by_cell(output_second)
    pair = jnp.concatenate((second_cells, by_cell(cotangent_first)), axis=-1)
    left, right = pair[:, 0:HALF], pair[:, HALF:WC]
    east = shifted(left, 0, -1)
    diag = shifted(left, -1, -1)
    south = shifted(right, -1, 0)

    first_row = lax.axis_index("lat") * WL
    meta = jnp.stack((shifts[0], lax.axis_size("lat") * WL - shifts[0] - first_row))
    gain = norm_gain.reshape(1, C)
    w_qkv_t = w_qkv.T

    table = pl.pallas_call(
        table_kernel,
        out_shape=jax.ShapeDtypeStruct((16, 16, LANES), f32),
        in_specs=vmem(1),
        out_specs=vmem(1)[0],
        scratch_shapes=[pltpu.VMEM((16, WIDE), f32), pltpu.VMEM((ROWS, LANES), f32)],
        compiler_params=params,
        cost_estimate=cost(400_000_000, 1_000_000),
        name="bias_table",
    )(earth_bias.reshape(2 * HEADS, 1, POS))

    piece = functools.partial(jax.ShapeDtypeStruct, dtype=bf16)
    half_block = (WL, HALF, LEVELS, 2 * C)
    own, to_east, bias_part = pl.pallas_call(
        main_kernel,
        out_shape=(piece(half_block), piece(half_block), piece((4 * HEADS, FOLD))),
        in_specs=smem() + vmem(9),
        out_specs=tuple(vmem(3)),
        scratch_shapes=[
            pltpu.VMEM((CELLS, 2 * C), f32),
            pltpu.VMEM((ROWS, LANES), f32),
            pltpu.VMEM((2, ROWS, C), bf16),
            pltpu.VMEM((2, ROWS, C), bf16),
            pltpu.VMEM((2, C, ROWS), bf16),
            pltpu.VMEM((2, C, ROWS), bf16),
            pltpu.VMEM((2, C, LANES), bf16),
            pltpu.VMEM((2, C, LANES), bf16),
            pltpu.VMEM((2, C, ROWS), bf16),
            pltpu.VMEM((2, C, ROWS), bf16),
            pltpu.VMEM((2, C, LANES), bf16),
            pltpu.VMEM((2, C, LANES), bf16),
            pltpu.VMEM((16, 16, LANES), f32),
            pltpu.VMEM((16, WIDE), f32),
            pltpu.VMEM((4 * HEADS, FOLD), f32),
        ],
        compiler_params=params,
        cost_estimate=cost(4_000_000_000, 2_000_000),
        name="window_attention",
    )(meta, right, east, south, diag, gain, w_qkv, w_qkv_t, w_proj, table)

    west = shifted(to_east, 0, 1)
    corner = shifted(to_east, 1, 1)
    north = shifted(own, 1, 0)

    steps = [("lon", 1 << bit) for bit in range((lax.axis_size("lon") - 1).bit_length())]
    steps += [("dp", 1 << bit) for bit in range((lax.axis_size("dp") - 1).bit_length())]
    for axis, stride in steps[:-1]:
        other = partner(bias_part, axis, stride)
        bias_part = (bias_part.astype(f32) + other.astype(f32)).astype(bf16)
    bias_grad = pl.pallas_call(
        table_home_kernel,
        out_shape=jax.ShapeDtypeStruct((2 * HEADS, 1, POS), f32),
        in_specs=vmem(2),
        out_specs=vmem(1)[0],
        compiler_params=params,
        cost_estimate=cost(100_000, 400_000),
        name="table_home",
    )(bias_part, partner(bias_part, *steps[-1]))

    block = jax.ShapeDtypeStruct((WL, WC, LEVELS, C), bf16)
    input_first, grad_second = pl.pallas_call(
        home_kernel,
        out_shape=(block, block),
        in_specs=smem() + vmem(9),
        out_specs=tuple(vmem(2)),
        scratch_shapes=[pltpu.VMEM((CELLS, 2 * C), f32)],
        compiler_params=params,
        cost_estimate=cost(200_000_000, 2_000_000),
        name="home",
    )(
        meta,
        own,
        west,
        north,
        corner,
        by_cell(output_first),
        second_cells,
        by_cell(cotangent_second),
        gain,
        w_proj,
    )
    return (
        input_first.transpose(2, 0, 1, 3)[None],
        grad_second.transpose(2, 0, 1, 3)[None],
        bias_grad.reshape(2, 1, HEADS, POS),
    )


def solution(mesh):
    block = P("dp", None, "lat", "lon", None)
    table = P(None, "lat", None, None)
    return jax.shard_map(
        local,
        mesh=mesh,
        in_specs=(block, block, block, block, P(), P(), P(), table, P(), P()),
        out_specs=(block, block, table),
        check_vma=False,
    )
```

```python
import functools

import jax
import jax.numpy as jnp
from jax import lax
from jax.experimental import pallas as pl
from jax.experimental.pallas import tpu as pltpu
from jax.sharding import PartitionSpec as P

C = 192
HEADS = 6
HEAD = 32
LEVELS = 4
WL = 6
WC = 12
HALF = 6
POS = 3312
CHUNK = 138
SPAN = 23
GROUPS = 12
ROWS = 192
LANES = 384
CELLS = 288
PITCH = 16
WIDE = 3584
FOLD = 1664
TILES = 78
CHUNKS = 16
DEEP = 5
SAMPLES = 2

norm_eps = 1e-05
mask_fill = -1e30
scale = HEAD**-0.5
vmem_bytes = 20 * 1024 * 1024

f32 = jnp.float32
bf16 = jnp.bfloat16


def iota(shape, dim):
    return lax.broadcasted_iota(jnp.int32, shape, dim)


def mm(a, b):
    return lax.dot_general(a, b, (((1,), (0,)), ((), ())), preferred_element_type=f32)


def mm_t(a, b):
    return lax.dot_general(a, b, (((1,), (1,)), ((), ())), preferred_element_type=f32)


def parts(index, size):
    return lax.div(index, jnp.int32(size)), lax.rem(index, jnp.int32(size))


def picks(index, count, dim):
    shape = (index.shape[0], count) if dim == 0 else (count, index.shape[1])
    return jnp.where(iota(shape, 1 - dim) == index, 1.0, 0.0).astype(bf16)


def line(size, dim):
    return iota((size, 1) if dim == 0 else (1, size), dim)


def query_cells(a, dim):
    column, group = parts(line(ROWS, dim), PITCH)
    level, row = parts(group, WL)
    return jnp.where(group < GROUPS, (row * WC + column) * LEVELS + 2 * a + level, -1)


def key_cells(a, dim):
    group, column = parts(line(LANES, dim), 32)
    level, row = parts(group, WL)
    return jnp.where(column < WC, (row * WC + column) * LEVELS + 2 * a + level, -1)


def spread_matrix(level, dim):
    group, place = parts(line(LANES, dim), 32)
    group = group - level * WL
    entry = jnp.where(
        (group >= 0) & (group < WL) & (place < SPAN), group * SPAN + place, -1
    )
    return picks(entry, LANES, dim)


def chunk_place(group, level):
    start = (((group // WL) * 2 + level) * WL + group % WL) * CHUNK
    return start // 128 * 128, start % 128


def table_kernel(bias_ref, gain_ref, table_ref, gain_out, wide, pieces):
    gain_out[...] = gain_ref[...]
    wide[...] = jnp.zeros(wide.shape, f32)
    for a in range(2):
        for h in range(HEADS):
            wide[a * 8 + h : a * 8 + h + 1, 0:POS] = bias_ref[a * HEADS + h]
    total = jnp.zeros((ROWS, LANES), f32)
    for level in range(2):
        for group in range(GROUPS):
            tile, shift = chunk_place(group, level)
            piece = wide[:, tile : tile + LANES]
            if shift:
                piece = pltpu.roll(piece, LANES - shift, 1)
            pieces[group * PITCH : (group + 1) * PITCH, :] = piece
        spread = spread_matrix(level, 1)
        rest = pieces[...]
        for _ in range(3):
            part = rest.astype(bf16)
            total = total + mm(part, spread)
            rest = rest - part.astype(f32)
    pieces[...] = total
    table_ref[...] = jnp.zeros(table_ref.shape, f32)
    for group in range(GROUPS):
        for place in range(16):
            row = group * PITCH + place
            table_ref[place, group : group + 1, :] = pieces[row : row + 1, :]


def frame_kernel(meta_ref, own_ref, other_ref, near_out, send_out):
    for r in range(WL):
        place = r + meta_ref[0]

        @pl.when(place < WL)
        def _():
            near_out[r] = own_ref[place, HALF:WC]
            send_out[r] = own_ref[place, 0:HALF]

        @pl.when(place >= WL)
        def _():
            near_out[r] = other_ref[place - WL, HALF:WC]
            send_out[r] = other_ref[place - WL, 0:HALF]


def unframe_kernel(meta_ref, own_ref, other_ref, near_out, send_out):
    for r in range(WL):
        place = r - meta_ref[0]

        @pl.when(place >= 0)
        def _():
            near_out[r] = own_ref[place, 0:HALF]
            send_out[r] = own_ref[place, HALF:WC]

        @pl.when(place < 0)
        def _():
            near_out[r] = other_ref[place + WL - 1, 0:HALF]
            send_out[r] = other_ref[place + WL - 1, HALF:WC]


def join_halves(left_ref, right_ref, joined):
    half = HALF * LEVELS
    for r in range(WL):
        start = 2 * r * half
        joined[start : start + half, :] = left_ref[r].astype(f32).reshape(half, 2 * C)
        joined[start + half : start + 2 * half, :] = (
            right_ref[r].astype(f32).reshape(half, 2 * C)
        )


def scores_kernel(
    meta_ref,
    near_ref,
    east_ref,
    gain_ref,
    w_qkv_ref,
    w_qkv_t_ref,
    w_proj_ref,
    table_ref,
    weights_out,
    grads_out,
    queries_t,
    ups_t,
    keys_t,
    values_t,
    bias_out,
    framed,
    mask,
    queries,
    ups,
    table_grad,
    wide,
    folds,
    packed_table,
):
    edge = meta_ref[1]
    join_halves(near_ref, east_ref, framed)

    cells = framed[:, 0:C]
    cotangent = framed[:, C : 2 * C].astype(bf16)
    centered = cells - jnp.mean(cells, axis=-1, keepdims=True)
    inverse = lax.rsqrt(jnp.mean(centered * centered, axis=-1, keepdims=True) + norm_eps)
    hidden = (centered * inverse * gain_ref[...]).astype(bf16)

    w_proj = w_proj_ref[...]
    for a in range(2):
        to_queries = picks(query_cells(a, 0), CELLS, 0)
        turned = mm(to_queries, hidden).astype(bf16)
        turned_cot = mm(to_queries, cotangent).astype(bf16)
        spaced = mm(picks(key_cells(a, 0), CELLS, 0), hidden).astype(bf16)
        queries[a] = mm(turned, w_qkv_ref[:, 0:C]).astype(bf16)
        queries_t[a] = mm_t(w_qkv_t_ref[0:C, :], turned).astype(bf16)
        keys_t[a] = mm_t(w_qkv_t_ref[C : 2 * C, :], spaced).astype(bf16)
        values_t[a] = mm_t(w_qkv_t_ref[2 * C : 3 * C, :], spaced).astype(bf16)
        ups[a] = mm_t(turned_cot, w_proj).astype(bf16)
        ups_t[a] = mm_t(w_proj, turned_cot).astype(bf16)

    query_row = parts(parts(line(ROWS, 0), PITCH)[1], WL)[1]
    key_group, key_column = parts(line(LANES, 1), 32)
    key_row = parts(key_group, WL)[1]
    query_id = jnp.where(query_row >= edge, 1, 0)
    key_id = jnp.where(key_column < WC, jnp.where(key_row >= edge, 1, 0), 2)
    mask[...] = jnp.where(query_id == key_id, 0.0, mask_fill)
    table_grad[...] = jnp.zeros(table_grad.shape, f32)

    def one_head(h, carry):
        chosen = iota((1, C), 1) // HEAD == h
        for a in range(2):
            query = jnp.where(chosen, queries[a], jnp.zeros((), bf16))
            up = jnp.where(chosen, ups[a], jnp.zeros((), bf16))
            scores = mm(query, keys_t[a]) * scale
            table = table_ref[a * 8 + h]
            bias = jnp.concatenate(
                [
                    pltpu.roll(table, (c - WC + 1) % LANES, 1) if c != WC - 1 else table
                    for c in range(WC)
                ],
                axis=0,
            )
            scores = scores + bias + mask[...]
            exponent = jnp.exp(scores - jnp.max(scores, axis=-1, keepdims=True))
            weights = exponent * (1.0 / jnp.sum(exponent, axis=-1, keepdims=True))
            weights_low = weights.astype(bf16)
            grad_weights = mm(up, values_t[a])
            row_dot = jnp.sum(weights * grad_weights, axis=-1, keepdims=True)
            grad_scores = weights * (grad_weights - row_dot)
            weights_out[a, h] = weights_low
            grads_out[a, h] = grad_scores.astype(bf16)
            folded = grad_scores[(WC - 1) * PITCH : WC * PITCH]
            for c in range(WC - 1):
                folded = folded + pltpu.roll(
                    grad_scores[c * PITCH : (c + 1) * PITCH], WC - 1 - c, 1
                )
            table_grad[a * 8 + h] = folded
        return carry

    lax.fori_loop(0, HEADS, one_head, 0)

    group, place = parts(line(ROWS, 0), PITCH)
    by_group = mm(
        picks(place * PITCH + group, 256, 0),
        table_grad[...].reshape(256, LANES).astype(bf16),
    ).astype(bf16)
    wide[...] = jnp.zeros(wide.shape, f32)
    for level in range(2):
        packed = mm(by_group, spread_matrix(level, 0))
        for group in range(GROUPS):
            tile, turn = chunk_place(group, level)
            piece = packed[group * PITCH : (group + 1) * PITCH]
            if turn:
                piece = pltpu.roll(piece, turn, 1)
            wide[:, tile : tile + LANES] += piece
    packed_table[...] = jnp.zeros(packed_table.shape, f32)
    for side in range(2):
        for a in range(2):
            start = (2 * side + a) * HEADS
            folds[start : start + HEADS, :] = wide[
                a * 8 : a * 8 + HEADS, side * FOLD : (side + 1) * FOLD
            ]
    for tile in range(TILES):
        chunk, slot, fold_rows, fold_lanes = tile_place(tile)
        packed_table[chunk, slot] = folds[fold_rows, fold_lanes]
    bias_out[...] = packed_table[...].astype(bf16)


def coeffs_kernel(
    weights_ref,
    grads_ref,
    queries_t,
    ups_t,
    keys_t,
    values_t,
    w_qkv_t_ref,
    own_out,
    south_out,
    attended_t,
    grad_query_t,
    grad_key_t,
    grad_value_t,
    joined,
):
    for h in range(HEADS):
        features = slice(h * HEAD, (h + 1) * HEAD)
        for a in range(2):
            weights_low = weights_ref[a, h]
            grad_low = grads_ref[a, h]
            attended_t[a, features, :] = mm_t(values_t[a, features, :], weights_low).astype(bf16)
            grad_value_t[a, features, :] = mm(ups_t[a, features, :], weights_low).astype(bf16)
            grad_query_t[a, features, :] = (
                mm_t(keys_t[a, features, :], grad_low) * scale
            ).astype(bf16)
            grad_key_t[a, features, :] = (
                mm(queries_t[a, features, :], grad_low) * scale
            ).astype(bf16)

    attended = jnp.zeros((CELLS, C), f32)
    coeffs = [jnp.zeros((CELLS, C), f32) for _ in range(3)]
    for a in range(2):
        from_queries = picks(query_cells(a, 1), CELLS, 1)
        from_keys = picks(key_cells(a, 1), CELLS, 1)
        attended = attended + mm_t(from_queries, attended_t[a])
        coeffs[0] = coeffs[0] + mm_t(from_queries, grad_query_t[a])
        coeffs[1] = coeffs[1] + mm_t(from_keys, grad_key_t[a])
        coeffs[2] = coeffs[2] + mm_t(from_keys, grad_value_t[a])
    joined[:, 0:C] = attended
    joined[:, C : 2 * C] = sum(
        mm(coeffs[part].astype(bf16), w_qkv_t_ref[part * C : (part + 1) * C, :])
        for part in range(3)
    )
    row_cells = WC * LEVELS
    for r in range(WL):
        row = joined[r * row_cells : (r + 1) * row_cells, :]
        row = row.reshape(WC, LEVELS, 2 * C).astype(bf16)
        own_out[r] = row
        if r:
            south_out[r - 1] = row


def home_kernel(
    west_ref,
    near_ref,
    output_first_ref,
    output_second_ref,
    cotangent_second_ref,
    gain_ref,
    w_proj_ref,
    input_first_out,
    grad_second_out,
    placed,
):
    join_halves(west_ref, near_ref, placed)
    shape = (WL, WC, LEVELS, C)
    mixed = mm(placed[:, 0:C].astype(bf16), w_proj_ref[...])
    first = output_first_ref[...].astype(f32).reshape(CELLS, C)
    input_first_out[...] = (first - mixed).reshape(shape).astype(bf16)

    cells = output_second_ref[...].astype(f32).reshape(CELLS, C)
    centered = cells - jnp.mean(cells, axis=-1, keepdims=True)
    inverse = lax.rsqrt(jnp.mean(centered * centered, axis=-1, keepdims=True) + norm_eps)
    normed = centered * inverse
    scaled = placed[:, C : 2 * C] * gain_ref[...]
    backward = inverse * (
        scaled
        - jnp.mean(scaled, axis=-1, keepdims=True)
        - normed * jnp.mean(scaled * normed, axis=-1, keepdims=True)
    )
    second = cotangent_second_ref[...].astype(f32).reshape(CELLS, C)
    grad_second_out[...] = (second + backward).reshape(shape).astype(bf16)


def tile_place(tile):
    chunk, slot = divmod(tile, DEEP)
    block, column = divmod(tile, FOLD // 128)
    return (
        chunk,
        slot,
        slice(block * 4, block * 4 + 4),
        slice(column * 128, column * 128 + 128),
    )


def table_sum_kernel(parts_ref, after_ref, sums_out):
    total = jnp.sum(parts_ref[...].astype(f32), axis=0).astype(bf16)
    for peer in range(sums_out.shape[0]):
        sums_out[peer] = total


def table_home_kernel(sums_ref, table_out, folds):
    for tile in range(TILES):
        chunk, slot, fold_rows, fold_lanes = tile_place(tile)
        samples = [
            sums_ref[chunk * SAMPLES + part, slot].astype(f32) for part in range(SAMPLES)
        ]
        folds[fold_rows, fold_lanes] = sum(samples)
    rows = 2 * HEADS
    for row in range(rows):
        table_out[row, :, 0:FOLD] = folds[row : row + 1]
        table_out[row, :, FOLD:POS] = folds[rows + row : rows + row + 1, 0 : POS - FOLD]


def vmem(count):
    return [pl.BlockSpec(memory_space=pltpu.VMEM)] * count


def smem():
    return [pl.BlockSpec(memory_space=pltpu.SMEM)]


params = pltpu.CompilerParams(vmem_limit_bytes=vmem_bytes)


def cost(flops, moved):
    return pl.CostEstimate(flops=flops, bytes_accessed=moved, transcendentals=0)


def shifted(x, axis, step):
    size = lax.axis_size(axis)
    return lax.ppermute(x, axis, [(i, (i + step) % size) for i in range(size)])


def every_peer(x, axes):
    return lax.all_to_all(x, axes, 0, 0, tiled=True)


def by_cell(x):
    return x[0].transpose(1, 2, 0, 3)


def local(
    output_first,
    output_second,
    cotangent_first,
    cotangent_second,
    norm_gain,
    w_qkv,
    w_proj,
    earth_bias,
    shifts,
    region,
):
    second_cells = by_cell(output_second)
    pair = jnp.concatenate((second_cells, by_cell(cotangent_first)), axis=-1)
    south = shifted(pair[0 : WL - 1], "lat", -1)

    first_row = lax.axis_index("lat") * WL
    meta = jnp.stack((shifts[0], lax.axis_size("lat") * WL - shifts[0] - first_row))
    w_qkv_t = w_qkv.T

    table, gain = pl.pallas_call(
        table_kernel,
        out_shape=(
            jax.ShapeDtypeStruct((16, 16, LANES), f32),
            jax.ShapeDtypeStruct((1, C), f32),
        ),
        in_specs=vmem(2),
        out_specs=tuple(vmem(2)),
        scratch_shapes=[pltpu.VMEM((16, WIDE), f32), pltpu.VMEM((ROWS, LANES), f32)],
        compiler_params=params,
        cost_estimate=cost(400_000_000, 1_000_000),
        name="bias_table",
    )(earth_bias.reshape(2 * HEADS, 1, POS), norm_gain.reshape(1, C))

    piece = functools.partial(jax.ShapeDtypeStruct, dtype=bf16)
    half_block = (WL, HALF, LEVELS, 2 * C)
    near, to_west = pl.pallas_call(
        frame_kernel,
        out_shape=(piece(half_block), piece(half_block)),
        in_specs=smem() + vmem(2),
        out_specs=tuple(vmem(2)),
        compiler_params=params,
        cost_estimate=cost(0, 500_000),
        name="frame_rows",
    )(meta, pair, south)
    east = shifted(to_west, "lon", -1)

    table_chunks = (CHUNKS, DEEP, 4, 128)
    *attention, bias_part = pl.pallas_call(
        scores_kernel,
        out_shape=(
            piece((2, HEADS, ROWS, LANES)),
            piece((2, HEADS, ROWS, LANES)),
            piece((2, C, ROWS)),
            piece((2, C, ROWS)),
            piece((2, C, LANES)),
            piece((2, C, LANES)),
            piece(table_chunks),
        ),
        in_specs=smem() + vmem(7),
        out_specs=tuple(vmem(7)),
        scratch_shapes=[
            pltpu.VMEM((CELLS, 2 * C), f32),
            pltpu.VMEM((ROWS, LANES), f32),
            pltpu.VMEM((2, ROWS, C), bf16),
            pltpu.VMEM((2, ROWS, C), bf16),
            pltpu.VMEM((16, 16, LANES), f32),
            pltpu.VMEM((16, WIDE), f32),
            pltpu.VMEM((4 * HEADS, FOLD), f32),
            pltpu.VMEM(table_chunks, f32),
        ],
        compiler_params=params,
        cost_estimate=cost(4_000_000_000, 2_000_000),
        name="window_scores",
    )(meta, near, east, gain, w_qkv, w_qkv_t, w_proj, table)

    own, to_south = pl.pallas_call(
        coeffs_kernel,
        out_shape=(
            piece((WL, WC, LEVELS, 2 * C)),
            piece((WL - 1, WC, LEVELS, 2 * C)),
        ),
        in_specs=vmem(7),
        out_specs=tuple(vmem(2)),
        scratch_shapes=[
            pltpu.VMEM((2, C, ROWS), bf16),
            pltpu.VMEM((2, C, ROWS), bf16),
            pltpu.VMEM((2, C, LANES), bf16),
            pltpu.VMEM((2, C, LANES), bf16),
            pltpu.VMEM((CELLS, 2 * C), f32),
        ],
        compiler_params=params,
        cost_estimate=cost(4_000_000_000, 2_000_000),
        name="window_coeffs",
    )(*attention, w_qkv_t)
    north = shifted(to_south, "lat", 1)

    sums = pl.pallas_call(
        table_sum_kernel,
        out_shape=piece((CHUNKS * SAMPLES, DEEP, 4, 128)),
        in_specs=vmem(1) + [pl.BlockSpec(memory_space=pl.ANY)],
        out_specs=vmem(1)[0],
        compiler_params=params,
        cost_estimate=cost(100_000, 400_000),
        name="table_sum",
    )(every_peer(bias_part, "lon"), north)
    bias_grad = pl.pallas_call(
        table_home_kernel,
        out_shape=jax.ShapeDtypeStruct((2 * HEADS, 1, POS), f32),
        in_specs=vmem(1),
        out_specs=vmem(1)[0],
        scratch_shapes=[pltpu.VMEM((4 * HEADS, FOLD), f32)],
        compiler_params=params,
        cost_estimate=cost(100_000, 400_000),
        name="table_home",
    )(every_peer(sums, ("lon", "dp")))

    near, to_east = pl.pallas_call(
        unframe_kernel,
        out_shape=(piece(half_block), piece(half_block)),
        in_specs=smem() + vmem(2),
        out_specs=tuple(vmem(2)),
        compiler_params=params,
        cost_estimate=cost(0, 500_000),
        name="home_rows",
    )(meta, own, north)
    west = shifted(to_east, "lon", 1)

    block = jax.ShapeDtypeStruct((WL, WC, LEVELS, C), bf16)
    input_first, grad_second = pl.pallas_call(
        home_kernel,
        out_shape=(block, block),
        in_specs=vmem(7),
        out_specs=tuple(vmem(2)),
        scratch_shapes=[pltpu.VMEM((CELLS, 2 * C), f32)],
        compiler_params=params,
        cost_estimate=cost(200_000_000, 2_000_000),
        name="home",
    )(
        west,
        near,
        by_cell(output_first),
        second_cells,
        by_cell(cotangent_second),
        gain,
        w_proj,
    )
    return (
        input_first.transpose(2, 0, 1, 3)[None],
        grad_second.transpose(2, 0, 1, 3)[None],
        bias_grad.reshape(2, 1, HEADS, POS),
    )


def solution(mesh):
    block = P("dp", None, "lat", "lon", None)
    table = P(None, "lat", None, None)
    return jax.shard_map(
        local,
        mesh=mesh,
        in_specs=(block, block, block, block, P(), P(), P(), table, P(), P()),
        out_specs=(block, block, table),
        check_vma=False,
    )
```

```python
import functools

import jax
import jax.numpy as jnp
from jax import lax
from jax.experimental import pallas as pl
from jax.experimental.pallas import tpu as pltpu
from jax.sharding import PartitionSpec as P

C = 192
HEADS = 6
HEAD = 32
LEVELS = 4
WL = 6
WC = 12
HALF = 6
POS = 3312
CHUNK = 138
SPAN = 23
GROUPS = 12
ROWS = 144
LANES = 256
REACH = 384
CELLS = 288
PITCH = 16
WIDE = 3584
FOLD = 1664
TILES = 156
CHUNKS = 32
DEEP = 5

norm_eps = 1e-05
mask_fill = -1e30
scale = HEAD**-0.5
vmem_bytes = 20 * 1024 * 1024

f32 = jnp.float32
bf16 = jnp.bfloat16


def iota(shape, dim):
    return lax.broadcasted_iota(jnp.int32, shape, dim)


def mm(a, b):
    return lax.dot_general(a, b, (((1,), (0,)), ((), ())), preferred_element_type=f32)


def mm_t(a, b):
    return lax.dot_general(a, b, (((1,), (1,)), ((), ())), preferred_element_type=f32)


def parts(index, size):
    return lax.div(index, jnp.int32(size)), lax.rem(index, jnp.int32(size))


def picks(index, count, dim):
    shape = (index.shape[0], count) if dim == 0 else (count, index.shape[1])
    return jnp.where(iota(shape, 1 - dim) == index, 1.0, 0.0).astype(bf16)


def line(size, dim):
    return iota((size, 1) if dim == 0 else (1, size), dim)


def query_cells(a, dim):
    column, group = parts(line(ROWS, dim), GROUPS)
    level, row = parts(group, WL)
    return (row * WC + column) * LEVELS + 2 * a + level


def key_cells(a, dim):
    group, column = parts(line(LANES, dim), PITCH)
    level, row = parts(group, WL)
    return jnp.where(
        (group < GROUPS) & (column < WC), (row * WC + column) * LEVELS + 2 * a + level, -1
    )


def spread_entries(level, part, dim):
    group, place = parts(line(LANES, dim), PITCH)
    group = group - level * WL - part
    count = SPAN - PITCH if part else PITCH
    return jnp.where(
        (group >= 0) & (group < WL) & (place < count),
        group * SPAN + place + part * PITCH,
        -1,
    )


def chunk_place(group, level):
    start = (((group // WL) * 2 + level) * WL + group % WL) * CHUNK
    return start // 128 * 128, start % 128


def table_kernel(
    shifts_ref, bias_ref, gain_ref, expanded_out, gain_out, wide, pieces, tables, mask
):
    gain_out[...] = gain_ref[...]
    wide[...] = jnp.zeros(wide.shape, f32)
    for a in range(2):
        for h in range(HEADS):
            wide[a * 8 + h : a * 8 + h + 1, 0:POS] = bias_ref[a * HEADS + h]
    totals = [jnp.zeros((GROUPS * PITCH, LANES), f32) for _ in range(2)]
    for level in range(2):
        for group in range(GROUPS):
            tile, shift = chunk_place(group, level)
            piece = wide[:, tile : tile + REACH]
            if shift:
                piece = pltpu.roll(piece, REACH - shift, 1)
            pieces[group * PITCH : (group + 1) * PITCH, :] = piece[:, 0:LANES]
        spreads = [picks(spread_entries(level, part, 1), LANES, 1) for part in range(2)]
        rest = pieces[...]
        for _ in range(3):
            top = rest.astype(bf16)
            for part in range(2):
                totals[part] = totals[part] + mm(top, spreads[part])
            rest = rest - top.astype(f32)
    for part in range(2):
        pieces[...] = totals[part]
        for group in range(GROUPS):
            for a in range(2):
                for h in range(HEADS):
                    row = group * PITCH + a * 8 + h
                    tables[part, a * HEADS + h, group : group + 1, :] = pieces[row : row + 1, :]

    first_row = lax.axis_index("lat") * WL
    edge = lax.axis_size("lat") * WL - shifts_ref[0] - first_row
    query_row = parts(line(GROUPS, 0), WL)[1]
    key_group, key_column = parts(line(LANES, 1), PITCH)
    key_row = parts(key_group, WL)[1]
    query_id = jnp.where(query_row >= edge, 1, 0)
    valid = (key_group < GROUPS) & (key_column < WC)
    key_id = jnp.where(valid, jnp.where(key_row >= edge, 1, 0), 2)
    mask[...] = jnp.where(query_id == key_id, 0.0, mask_fill)

    def expand(index, carry):
        first, second = tables[0, index], tables[1, index]
        for c in range(WC):
            shift = (c - WC + 1) % LANES
            low = pltpu.roll(first, shift, 1) if shift else first
            high = pltpu.roll(second, shift, 1) if shift else second
            bias = jnp.where(key_column + (WC - 1 - c) < PITCH, low, high)
            expanded_out[index, c * GROUPS : (c + 1) * GROUPS, :] = bias + mask[...]
        return carry

    lax.fori_loop(0, 2 * HEADS, expand, 0)


def unframe_kernel(shifts_ref, own_ref, other_ref, near_out, send_out):
    for r in range(WL):
        place = r - shifts_ref[0]

        @pl.when(place >= 0)
        def _():
            near_out[r] = own_ref[place, 0:HALF]
            send_out[r] = own_ref[place, HALF:WC]

        @pl.when(place < 0)
        def _():
            near_out[r] = other_ref[place + WL - 1, 0:HALF]
            send_out[r] = other_ref[place + WL - 1, HALF:WC]


def join_halves(left_ref, right_ref, joined):
    half = HALF * LEVELS
    for r in range(WL):
        start = 2 * r * half
        joined[start : start + half, :] = left_ref[r].astype(f32).reshape(half, 2 * C)
        joined[start + half : start + 2 * half, :] = (
            right_ref[r].astype(f32).reshape(half, 2 * C)
        )


def attention_kernel(
    shifts_ref,
    own_ref,
    east_ref,
    south_ref,
    diag_ref,
    gain_ref,
    w_qkv_ref,
    w_qkv_t_ref,
    w_proj_ref,
    bias_ref,
    own_out,
    south_out,
    bias_out,
    framed,
    queries,
    ups,
    queries_t,
    ups_t,
    keys_t,
    values_t,
    attended_t,
    grad_query_t,
    grad_key_t,
    grad_value_t,
    table_grad,
    wide,
    folds,
    packed_table,
):
    half = HALF * LEVELS
    for r in range(WL):
        place = r + shifts_ref[0]
        left = slice(2 * r * half, (2 * r + 1) * half)
        right = slice((2 * r + 1) * half, (2 * r + 2) * half)

        @pl.when(place < WL)
        def _():
            framed[left, :] = own_ref[place].astype(f32).reshape(half, 2 * C)
            framed[right, :] = east_ref[place].astype(f32).reshape(half, 2 * C)

        @pl.when(place >= WL)
        def _():
            framed[left, :] = south_ref[place - WL].astype(f32).reshape(half, 2 * C)
            framed[right, :] = diag_ref[place - WL].astype(f32).reshape(half, 2 * C)

    cells = framed[:, 0:C]
    cotangent = framed[:, C : 2 * C].astype(bf16)
    centered = cells - jnp.mean(cells, axis=-1, keepdims=True)
    inverse = lax.rsqrt(jnp.mean(centered * centered, axis=-1, keepdims=True) + norm_eps)
    hidden = (centered * inverse * gain_ref[...]).astype(bf16)

    w_proj = w_proj_ref[...]
    for a in range(2):
        to_queries = picks(query_cells(a, 0), CELLS, 0)
        turned = mm(to_queries, hidden).astype(bf16)
        turned_cot = mm(to_queries, cotangent).astype(bf16)
        spaced = mm(picks(key_cells(a, 0), CELLS, 0), hidden).astype(bf16)
        queries[a] = mm(turned, w_qkv_ref[:, 0:C]).astype(bf16)
        queries_t[a] = mm_t(w_qkv_t_ref[0:C, :], turned).astype(bf16)
        keys_t[a] = mm_t(w_qkv_t_ref[C : 2 * C, :], spaced).astype(bf16)
        values_t[a] = mm_t(w_qkv_t_ref[2 * C : 3 * C, :], spaced).astype(bf16)
        ups[a] = mm_t(turned_cot, w_proj).astype(bf16)
        ups_t[a] = mm_t(w_proj, turned_cot).astype(bf16)

    table_grad[...] = jnp.zeros(table_grad.shape, f32)
    key_column = parts(line(LANES, 1), PITCH)[1]

    def one_head(h, carry):
        features = pl.ds(pl.multiple_of(h * HEAD, HEAD), HEAD)
        chosen = parts(line(C, 1), HEAD)[0] == h
        for a in range(2):
            query = jnp.where(chosen, queries[a], jnp.zeros((), bf16))
            up = jnp.where(chosen, ups[a], jnp.zeros((), bf16))
            scores = mm(query, keys_t[a]) * scale + bias_ref[a * HEADS + h]
            exponent = jnp.exp(scores - jnp.max(scores, axis=-1, keepdims=True))
            weights = exponent * (1.0 / jnp.sum(exponent, axis=-1, keepdims=True))
            weights_low = weights.astype(bf16)
            grad_weights = mm(up, values_t[a])
            row_dot = jnp.sum(weights * grad_weights, axis=-1, keepdims=True)
            grad_scores = weights * (grad_weights - row_dot)
            grad_low = grad_scores.astype(bf16)
            attended_t[a, features, :] = mm_t(values_t[a, features, :], weights_low).astype(bf16)
            grad_value_t[a, features, :] = mm(ups_t[a, features, :], weights_low).astype(bf16)
            grad_query_t[a, features, :] = (
                mm_t(keys_t[a, features, :], grad_low) * scale
            ).astype(bf16)
            grad_key_t[a, features, :] = (
                mm(queries_t[a, features, :], grad_low) * scale
            ).astype(bf16)
            low = jnp.zeros((GROUPS, LANES), f32)
            high = jnp.zeros((GROUPS, LANES), f32)
            for c in range(WC):
                shift = WC - 1 - c
                turned_grad = grad_scores[c * GROUPS : (c + 1) * GROUPS]
                if shift:
                    turned_grad = pltpu.roll(turned_grad, shift, 1)
                kept = key_column >= shift
                low = low + jnp.where(kept, turned_grad, 0.0)
                high = high + jnp.where(kept, 0.0, turned_grad)
            table_grad[0, a * 8 + h, 0:GROUPS] = low
            table_grad[1, a * 8 + h, 0:GROUPS] = high
        return carry

    lax.fori_loop(0, HEADS, one_head, 0)

    group, place = parts(line(GROUPS * PITCH, 0), PITCH)
    to_groups = picks(place * PITCH + group, 256, 0)
    by_group = [
        mm(to_groups, table_grad[part].reshape(256, LANES).astype(bf16)).astype(bf16)
        for part in range(2)
    ]
    wide[...] = jnp.zeros(wide.shape, f32)
    for level in range(2):
        packed = sum(
            mm(by_group[part], picks(spread_entries(level, part, 0), REACH, 0))
            for part in range(2)
        )
        for group in range(GROUPS):
            tile, turn = chunk_place(group, level)
            piece = packed[group * PITCH : (group + 1) * PITCH]
            if turn:
                piece = pltpu.roll(piece, turn, 1)
            wide[:, tile : tile + REACH] += piece
    packed_table[...] = jnp.zeros(packed_table.shape, f32)
    for side in range(2):
        for a in range(2):
            start = (2 * side + a) * HEADS
            folds[start : start + HEADS, :] = wide[
                a * 8 : a * 8 + HEADS, side * FOLD : (side + 1) * FOLD
            ]
    for tile in range(TILES):
        chunk, slot, fold_rows, fold_lanes = tile_place(tile)
        packed_table[chunk, slot] = folds[fold_rows, fold_lanes]
    bias_out[...] = packed_table[...].astype(bf16)

    attended = jnp.zeros((CELLS, C), f32)
    coeffs = [jnp.zeros((CELLS, C), f32) for _ in range(3)]
    for a in range(2):
        from_queries = picks(query_cells(a, 1), CELLS, 1)
        from_keys = picks(key_cells(a, 1), CELLS, 1)
        attended = attended + mm_t(from_queries, attended_t[a])
        coeffs[0] = coeffs[0] + mm_t(from_queries, grad_query_t[a])
        coeffs[1] = coeffs[1] + mm_t(from_keys, grad_key_t[a])
        coeffs[2] = coeffs[2] + mm_t(from_keys, grad_value_t[a])
    framed[:, 0:C] = attended
    framed[:, C : 2 * C] = sum(
        mm(coeffs[part].astype(bf16), w_qkv_t_ref[part * C : (part + 1) * C, :])
        for part in range(3)
    )
    row_cells = WC * LEVELS
    for r in range(WL):
        row = framed[r * row_cells : (r + 1) * row_cells, :]
        row = row.reshape(WC, LEVELS, 2 * C).astype(bf16)
        own_out[r] = row
        if r:
            south_out[r - 1] = row


def home_kernel(
    west_ref,
    near_ref,
    output_first_ref,
    output_second_ref,
    cotangent_second_ref,
    gain_ref,
    w_proj_ref,
    input_first_out,
    grad_second_out,
    placed,
):
    join_halves(west_ref, near_ref, placed)
    shape = (WL, WC, LEVELS, C)
    mixed = mm(placed[:, 0:C].astype(bf16), w_proj_ref[...])
    first = output_first_ref[...].astype(f32).reshape(CELLS, C)
    input_first_out[...] = (first - mixed).reshape(shape).astype(bf16)

    cells = output_second_ref[...].astype(f32).reshape(CELLS, C)
    centered = cells - jnp.mean(cells, axis=-1, keepdims=True)
    inverse = lax.rsqrt(jnp.mean(centered * centered, axis=-1, keepdims=True) + norm_eps)
    normed = centered * inverse
    scaled = placed[:, C : 2 * C] * gain_ref[...]
    backward = inverse * (
        scaled
        - jnp.mean(scaled, axis=-1, keepdims=True)
        - normed * jnp.mean(scaled * normed, axis=-1, keepdims=True)
    )
    second = cotangent_second_ref[...].astype(f32).reshape(CELLS, C)
    grad_second_out[...] = (second + backward).reshape(shape).astype(bf16)


def tile_place(tile):
    chunk, slot = divmod(tile, DEEP)
    block, column = divmod(tile, FOLD // 128)
    return (
        chunk,
        slot,
        slice(block * 2, block * 2 + 2),
        slice(column * 128, column * 128 + 128),
    )


def table_sum_kernel(parts_ref, after_ref, sums_out):
    total = jnp.sum(parts_ref[...].astype(f32), axis=0).astype(bf16)
    for peer in range(CHUNKS):
        sums_out[peer] = total


def table_home_kernel(sums_ref, table_out, folds):
    for tile in range(TILES):
        chunk, slot, fold_rows, fold_lanes = tile_place(tile)
        folds[fold_rows, fold_lanes] = sums_ref[chunk, slot].astype(f32)
    rows = 2 * HEADS
    for row in range(rows):
        table_out[row, :, 0:FOLD] = folds[row : row + 1]
        table_out[row, :, FOLD:POS] = folds[rows + row : rows + row + 1, 0 : POS - FOLD]


def vmem(count):
    return [pl.BlockSpec(memory_space=pltpu.VMEM)] * count


def smem():
    return [pl.BlockSpec(memory_space=pltpu.SMEM)]


params = pltpu.CompilerParams(vmem_limit_bytes=vmem_bytes)


def cost(flops, moved):
    return pl.CostEstimate(flops=flops, bytes_accessed=moved, transcendentals=0)


def shifted(x, axis, step):
    size = lax.axis_size(axis)
    return lax.ppermute(x, axis, [(i, (i + step) % size) for i in range(size)])


def from_diagonal(x):
    lons, lats = lax.axis_size("lon"), lax.axis_size("lat")
    pairs = [
        (i * lats + j, (i - 1) % lons * lats + (j - 1) % lats)
        for i in range(lons)
        for j in range(lats)
    ]
    return lax.ppermute(x, ("lon", "lat"), pairs)


def every_peer(x):
    return lax.all_to_all(x, ("lon", "dp"), 0, 0, tiled=True)


def by_cell(x):
    return x[0].transpose(1, 2, 0, 3)


def local(
    output_first,
    output_second,
    cotangent_first,
    cotangent_second,
    norm_gain,
    w_qkv,
    w_proj,
    earth_bias,
    shifts,
    region,
):
    second_cells = by_cell(output_second)
    pair = jnp.concatenate((second_cells, by_cell(cotangent_first)), axis=-1)
    left, right = pair[:, 0:HALF], pair[:, HALF:WC]
    east = shifted(left, "lon", -1)
    diag = from_diagonal(left)
    south = shifted(right, "lat", -1)

    w_qkv_t = w_qkv.T

    bias, gain = pl.pallas_call(
        table_kernel,
        out_shape=(
            jax.ShapeDtypeStruct((2 * HEADS, ROWS, LANES), f32),
            jax.ShapeDtypeStruct((1, C), f32),
        ),
        in_specs=smem() + vmem(2),
        out_specs=tuple(vmem(2)),
        scratch_shapes=[
            pltpu.VMEM((16, WIDE), f32),
            pltpu.VMEM((GROUPS * PITCH, LANES), f32),
            pltpu.VMEM((2, 2 * HEADS, GROUPS, LANES), f32),
            pltpu.VMEM((GROUPS, LANES), f32),
        ],
        compiler_params=params,
        cost_estimate=cost(400_000_000, 2_000_000),
        name="bias_table",
    )(shifts, earth_bias.reshape(2 * HEADS, 1, POS), norm_gain.reshape(1, C))

    piece = functools.partial(jax.ShapeDtypeStruct, dtype=bf16)
    table_chunks = (CHUNKS, DEEP, 2, 128)
    own, to_south, bias_part = pl.pallas_call(
        attention_kernel,
        out_shape=(
            piece((WL, WC, LEVELS, 2 * C)),
            piece((WL - 1, WC, LEVELS, 2 * C)),
            piece(table_chunks),
        ),
        in_specs=smem() + vmem(9),
        out_specs=tuple(vmem(3)),
        scratch_shapes=[
            pltpu.VMEM((CELLS, 2 * C), f32),
            pltpu.VMEM((2, ROWS, C), bf16),
            pltpu.VMEM((2, ROWS, C), bf16),
            pltpu.VMEM((2, C, ROWS), bf16),
            pltpu.VMEM((2, C, ROWS), bf16),
            pltpu.VMEM((2, C, LANES), bf16),
            pltpu.VMEM((2, C, LANES), bf16),
            pltpu.VMEM((2, C, ROWS), bf16),
            pltpu.VMEM((2, C, ROWS), bf16),
            pltpu.VMEM((2, C, LANES), bf16),
            pltpu.VMEM((2, C, LANES), bf16),
            pltpu.VMEM((2, 16, 16, LANES), f32),
            pltpu.VMEM((16, WIDE), f32),
            pltpu.VMEM((4 * HEADS, FOLD), f32),
            pltpu.VMEM(table_chunks, f32),
        ],
        compiler_params=params,
        cost_estimate=cost(4_000_000_000, 2_000_000),
        name="window_attention",
    )(shifts, right, east, south, diag, gain, w_qkv, w_qkv_t, w_proj, bias)
    north = shifted(to_south, "lat", 1)

    half_block = (WL, HALF, LEVELS, 2 * C)
    near, to_east = pl.pallas_call(
        unframe_kernel,
        out_shape=(piece(half_block), piece(half_block)),
        in_specs=smem() + vmem(2),
        out_specs=tuple(vmem(2)),
        compiler_params=params,
        cost_estimate=cost(20_000_000_000, 500_000),
        name="home_rows",
    )(shifts, own, north)
    west = shifted(to_east, "lon", 1)

    sums = pl.pallas_call(
        table_sum_kernel,
        out_shape=piece(table_chunks),
        in_specs=vmem(1) + [pl.BlockSpec(memory_space=pl.ANY)],
        out_specs=vmem(1)[0],
        compiler_params=params,
        cost_estimate=cost(100_000, 400_000),
        name="table_sum",
    )(every_peer(bias_part), near)
    bias_grad = pl.pallas_call(
        table_home_kernel,
        out_shape=jax.ShapeDtypeStruct((2 * HEADS, 1, POS), f32),
        in_specs=vmem(1),
        out_specs=vmem(1)[0],
        scratch_shapes=[pltpu.VMEM((4 * HEADS, FOLD), f32)],
        compiler_params=params,
        cost_estimate=cost(100_000, 400_000),
        name="table_home",
    )(every_peer(sums))

    block = jax.ShapeDtypeStruct((WL, WC, LEVELS, C), bf16)
    input_first, grad_second = pl.pallas_call(
        home_kernel,
        out_shape=(block, block),
        in_specs=vmem(7),
        out_specs=tuple(vmem(2)),
        scratch_shapes=[pltpu.VMEM((CELLS, 2 * C), f32)],
        compiler_params=params,
        cost_estimate=cost(20_000_000_000, 2_000_000),
        name="home",
    )(
        west,
        near,
        by_cell(output_first),
        second_cells,
        by_cell(cotangent_second),
        gain,
        w_proj,
    )
    return (
        input_first.transpose(2, 0, 1, 3)[None],
        grad_second.transpose(2, 0, 1, 3)[None],
        bias_grad.reshape(2, 1, HEADS, POS),
    )


def solution(mesh):
    block = P("dp", None, "lat", "lon", None)
    table = P(None, "lat", None, None)
    return jax.shard_map(
        local,
        mesh=mesh,
        in_specs=(block, block, block, block, P(), P(), P(), table, P(), P()),
        out_specs=(block, block, table),
        check_vma=False,
    )
```

```python
import functools

import jax
import jax.numpy as jnp
from jax import lax
from jax.experimental import pallas as pl
from jax.experimental.pallas import tpu as pltpu
from jax.sharding import PartitionSpec as P

C = 192
HEADS = 6
HEAD = 32
LEVELS = 4
WL = 6
WC = 12
HALF = 6
POS = 3312
CHUNK = 138
SPAN = 23
GROUPS = 12
ROWS = 144
LANES = 256
REACH = 384
CELLS = 288
PITCH = 16
WIDE = 3584
TILES = 156
CHUNKS = 32
DEEP = 5

norm_eps = 1e-05
mask_fill = -1e30
scale = HEAD**-0.5
vmem_bytes = 20 * 1024 * 1024

f32 = jnp.float32
bf16 = jnp.bfloat16


def iota(shape, dim):
    return lax.broadcasted_iota(jnp.int32, shape, dim)


def mm(a, b):
    return lax.dot_general(a, b, (((1,), (0,)), ((), ())), preferred_element_type=f32)


def mm_t(a, b):
    return lax.dot_general(a, b, (((1,), (1,)), ((), ())), preferred_element_type=f32)


def parts(index, size):
    return lax.div(index, jnp.int32(size)), lax.rem(index, jnp.int32(size))


def picks(index, count, dim):
    shape = (index.shape[0], count) if dim == 0 else (count, index.shape[1])
    return jnp.where(iota(shape, 1 - dim) == index, 1.0, 0.0).astype(bf16)


def line(size, dim):
    return iota((size, 1) if dim == 0 else (1, size), dim)


def query_cells(a, dim):
    column, group = parts(line(ROWS, dim), GROUPS)
    level, row = parts(group, WL)
    return (row * WC + column) * LEVELS + 2 * a + level


def key_cells(a, dim):
    group, column = parts(line(LANES, dim), PITCH)
    level, row = parts(group, WL)
    return jnp.where(
        (group < GROUPS) & (column < WC), (row * WC + column) * LEVELS + 2 * a + level, -1
    )


def spread_entries(level, part, dim):
    group, place = parts(line(LANES, dim), PITCH)
    group = group - level * WL - part
    count = SPAN - PITCH if part else PITCH
    return jnp.where(
        (group >= 0) & (group < WL) & (place < count),
        group * SPAN + place + part * PITCH,
        -1,
    )


def chunk_place(group, level):
    start = (((group // WL) * 2 + level) * WL + group % WL) * CHUNK
    return start // 128 * 128, start % 128


def table_kernel(
    shifts_ref, bias_ref, gain_ref, expanded_out, gain_out, wide, pieces, tables, mask
):
    gain_out[...] = gain_ref[...]
    wide[...] = jnp.zeros(wide.shape, f32)
    for a in range(2):
        for h in range(HEADS):
            wide[a * 8 + h : a * 8 + h + 1, 0:POS] = bias_ref[a * HEADS + h]
    totals = [jnp.zeros((GROUPS * PITCH, LANES), f32) for _ in range(2)]
    for level in range(2):
        for group in range(GROUPS):
            tile, shift = chunk_place(group, level)
            piece = wide[:, tile : tile + REACH]
            if shift:
                piece = pltpu.roll(piece, REACH - shift, 1)
            pieces[group * PITCH : (group + 1) * PITCH, :] = piece[:, 0:LANES]
        spreads = [picks(spread_entries(level, part, 1), LANES, 1) for part in range(2)]
        rest = pieces[...]
        for _ in range(3):
            top = rest.astype(bf16)
            for part in range(2):
                totals[part] = totals[part] + mm(top, spreads[part])
            rest = rest - top.astype(f32)
    for part in range(2):
        pieces[...] = totals[part]
        for group in range(GROUPS):
            for a in range(2):
                for h in range(HEADS):
                    row = group * PITCH + a * 8 + h
                    tables[part, a * HEADS + h, group : group + 1, :] = pieces[row : row + 1, :]

    first_row = lax.axis_index("lat") * WL
    edge = lax.axis_size("lat") * WL - shifts_ref[0] - first_row
    query_row = parts(line(GROUPS, 0), WL)[1]
    key_group, key_column = parts(line(LANES, 1), PITCH)
    key_row = parts(key_group, WL)[1]
    query_id = jnp.where(query_row >= edge, 1, 0)
    valid = (key_group < GROUPS) & (key_column < WC)
    key_id = jnp.where(valid, jnp.where(key_row >= edge, 1, 0), 2)
    mask[...] = jnp.where(query_id == key_id, 0.0, mask_fill)

    def expand(index, carry):
        first, second = tables[0, index], tables[1, index]
        for c in range(WC):
            shift = (c - WC + 1) % LANES
            low = pltpu.roll(first, shift, 1) if shift else first
            high = pltpu.roll(second, shift, 1) if shift else second
            bias = jnp.where(key_column + (WC - 1 - c) < PITCH, low, high)
            expanded_out[index, c * GROUPS : (c + 1) * GROUPS, :] = bias + mask[...]
        return carry

    lax.fori_loop(0, 2 * HEADS, expand, 0)


def unframe_kernel(shifts_ref, own_ref, other_ref, near_out, send_out):
    for r in range(WL):
        place = r - shifts_ref[0]

        @pl.when(place >= 0)
        def _():
            near_out[r] = own_ref[place, 0:HALF]
            send_out[r] = own_ref[place, HALF:WC]

        @pl.when(place < 0)
        def _():
            near_out[r] = other_ref[place + WL - 1, 0:HALF]
            send_out[r] = other_ref[place + WL - 1, HALF:WC]


def join_halves(left_ref, right_ref, joined):
    half = HALF * LEVELS
    for r in range(WL):
        start = 2 * r * half
        joined[start : start + half, :] = left_ref[r].astype(f32).reshape(half, 2 * C)
        joined[start + half : start + 2 * half, :] = (
            right_ref[r].astype(f32).reshape(half, 2 * C)
        )


def attention_kernel(
    shifts_ref,
    own_ref,
    east_ref,
    south_ref,
    diag_ref,
    gain_ref,
    w_qkv_ref,
    w_qkv_t_ref,
    w_proj_ref,
    bias_ref,
    own_out,
    south_out,
    bias_out,
    framed,
    queries,
    ups,
    queries_t,
    ups_t,
    keys_t,
    values_t,
    weights_low,
    grads_low,
    attended_t,
    grad_query_t,
    grad_key_t,
    grad_value_t,
    table_grad,
    wide,
    packed_table,
):
    half = HALF * LEVELS
    for r in range(WL):
        place = r + shifts_ref[0]
        left = slice(2 * r * half, (2 * r + 1) * half)
        right = slice((2 * r + 1) * half, (2 * r + 2) * half)

        @pl.when(place < WL)
        def _():
            framed[left, :] = own_ref[place].astype(f32).reshape(half, 2 * C)
            framed[right, :] = east_ref[place].astype(f32).reshape(half, 2 * C)

        @pl.when(place >= WL)
        def _():
            framed[left, :] = south_ref[place - WL].astype(f32).reshape(half, 2 * C)
            framed[right, :] = diag_ref[place - WL].astype(f32).reshape(half, 2 * C)

    cells = framed[:, 0:C]
    cotangent = framed[:, C : 2 * C].astype(bf16)
    centered = cells - jnp.mean(cells, axis=-1, keepdims=True)
    inverse = lax.rsqrt(jnp.mean(centered * centered, axis=-1, keepdims=True) + norm_eps)
    hidden = (centered * inverse * gain_ref[...]).astype(bf16)

    w_proj = w_proj_ref[...]
    for a in range(2):
        to_queries = picks(query_cells(a, 0), CELLS, 0)
        turned = mm(to_queries, hidden).astype(bf16)
        turned_cot = mm(to_queries, cotangent).astype(bf16)
        spaced = mm(picks(key_cells(a, 0), CELLS, 0), hidden).astype(bf16)
        queries[a] = mm(turned, w_qkv_ref[:, 0:C]).astype(bf16)
        queries_t[a] = mm_t(w_qkv_t_ref[0:C, :], turned).astype(bf16)
        keys_t[a] = mm_t(w_qkv_t_ref[C : 2 * C, :], spaced).astype(bf16)
        values_t[a] = mm_t(w_qkv_t_ref[2 * C : 3 * C, :], spaced).astype(bf16)
        ups[a] = mm_t(turned_cot, w_proj).astype(bf16)
        ups_t[a] = mm_t(w_proj, turned_cot).astype(bf16)

    table_grad[...] = jnp.zeros(table_grad.shape, f32)
    key_column = parts(line(LANES, 1), PITCH)[1]

    def one_head(h, carry):
        chosen = parts(line(C, 1), HEAD)[0] == h
        for a in range(2):
            query = jnp.where(chosen, queries[a], jnp.zeros((), bf16))
            up = jnp.where(chosen, ups[a], jnp.zeros((), bf16))
            scores = mm(query, keys_t[a]) * scale + bias_ref[a * HEADS + h]
            exponent = jnp.exp(scores - jnp.max(scores, axis=-1, keepdims=True))
            weights = exponent * (1.0 / jnp.sum(exponent, axis=-1, keepdims=True))
            grad_weights = mm(up, values_t[a])
            row_dot = jnp.sum(weights * grad_weights, axis=-1, keepdims=True)
            grad_scores = weights * (grad_weights - row_dot)
            weights_low[a, h] = weights.astype(bf16)
            grads_low[a, h] = grad_scores.astype(bf16)
            low = jnp.zeros((GROUPS, LANES), f32)
            high = jnp.zeros((GROUPS, LANES), f32)
            for c in range(WC):
                shift = WC - 1 - c
                turned_grad = grad_scores[c * GROUPS : (c + 1) * GROUPS]
                if shift:
                    turned_grad = pltpu.roll(turned_grad, shift, 1)
                kept = key_column >= shift
                low = low + jnp.where(kept, turned_grad, 0.0)
                high = high + jnp.where(kept, 0.0, turned_grad)
            table_grad[0, a * 8 + h, 0:GROUPS] = low
            table_grad[1, a * 8 + h, 0:GROUPS] = high
        return carry

    lax.fori_loop(0, HEADS, one_head, 0)

    group, place = parts(line(GROUPS * PITCH, 0), PITCH)
    to_groups = picks(place * PITCH + group, 256, 0)
    by_group = [
        mm(to_groups, table_grad[part].reshape(256, LANES).astype(bf16)).astype(bf16)
        for part in range(2)
    ]
    wide[...] = jnp.zeros(wide.shape, f32)
    for level in range(2):
        packed = sum(
            mm(by_group[part], picks(spread_entries(level, part, 0), REACH, 0))
            for part in range(2)
        )
        for group in range(GROUPS):
            tile, turn = chunk_place(group, level)
            piece = packed[group * PITCH : (group + 1) * PITCH]
            if turn:
                piece = pltpu.roll(piece, turn, 1)
            wide[:, tile : tile + REACH] += piece
    packed_table[...] = jnp.zeros(packed_table.shape, f32)
    for tile in range(TILES):
        chunk, slot, row, lanes = tile_place(tile)
        row = row // HEADS * 8 + row % HEADS
        packed_table[chunk, slot] = wide[row : row + 2, lanes]
    bias_out[...] = packed_table[...].astype(bf16)

    for h in range(HEADS):
        features = slice(h * HEAD, (h + 1) * HEAD)
        for a in range(2):
            weight, grad = weights_low[a, h], grads_low[a, h]
            attended_t[a, features, :] = mm_t(values_t[a, features, :], weight).astype(bf16)
            grad_value_t[a, features, :] = mm(ups_t[a, features, :], weight).astype(bf16)
            grad_query_t[a, features, :] = (
                mm_t(keys_t[a, features, :], grad) * scale
            ).astype(bf16)
            grad_key_t[a, features, :] = (
                mm(queries_t[a, features, :], grad) * scale
            ).astype(bf16)

    attended = jnp.zeros((CELLS, C), f32)
    coeffs = [jnp.zeros((CELLS, C), f32) for _ in range(3)]
    for a in range(2):
        from_queries = picks(query_cells(a, 1), CELLS, 1)
        from_keys = picks(key_cells(a, 1), CELLS, 1)
        attended = attended + mm_t(from_queries, attended_t[a])
        coeffs[0] = coeffs[0] + mm_t(from_queries, grad_query_t[a])
        coeffs[1] = coeffs[1] + mm_t(from_keys, grad_key_t[a])
        coeffs[2] = coeffs[2] + mm_t(from_keys, grad_value_t[a])
    framed[:, 0:C] = attended
    framed[:, C : 2 * C] = sum(
        mm(coeffs[part].astype(bf16), w_qkv_t_ref[part * C : (part + 1) * C, :])
        for part in range(3)
    )
    row_cells = WC * LEVELS
    for r in range(WL):
        row = framed[r * row_cells : (r + 1) * row_cells, :]
        row = row.reshape(WC, LEVELS, 2 * C).astype(bf16)
        own_out[r] = row
        if r:
            south_out[r - 1] = row


def home_kernel(
    west_ref,
    near_ref,
    output_first_ref,
    output_second_ref,
    cotangent_second_ref,
    gain_ref,
    w_proj_ref,
    input_first_out,
    grad_second_out,
    placed,
):
    join_halves(west_ref, near_ref, placed)
    shape = (WL, WC, LEVELS, C)
    mixed = mm(placed[:, 0:C].astype(bf16), w_proj_ref[...])
    first = output_first_ref[...].astype(f32).reshape(CELLS, C)
    input_first_out[...] = (first - mixed).reshape(shape).astype(bf16)

    cells = output_second_ref[...].astype(f32).reshape(CELLS, C)
    centered = cells - jnp.mean(cells, axis=-1, keepdims=True)
    inverse = lax.rsqrt(jnp.mean(centered * centered, axis=-1, keepdims=True) + norm_eps)
    normed = centered * inverse
    scaled = placed[:, C : 2 * C] * gain_ref[...]
    backward = inverse * (
        scaled
        - jnp.mean(scaled, axis=-1, keepdims=True)
        - normed * jnp.mean(scaled * normed, axis=-1, keepdims=True)
    )
    second = cotangent_second_ref[...].astype(f32).reshape(CELLS, C)
    grad_second_out[...] = (second + backward).reshape(shape).astype(bf16)


def tile_place(tile):
    chunk, slot = divmod(tile, DEEP)
    pair, column = divmod(tile, TILES // HEADS)
    return chunk, slot, 2 * pair, slice(column * 128, column * 128 + 128)


def table_sum_kernel(parts_ref, after_ref, sums_out):
    total = jnp.sum(parts_ref[...].astype(f32), axis=0).astype(bf16)
    for peer in range(CHUNKS):
        sums_out[peer] = total


def table_home_kernel(sums_ref, table_out):
    for tile in range(TILES):
        chunk, slot, row, lanes = tile_place(tile)
        sums = sums_ref[chunk, slot].astype(f32)
        width = min(128, POS - lanes.start)
        for place in range(2):
            table_out[row + place, :, lanes.start : lanes.start + width] = sums[
                place : place + 1, 0:width
            ]


def vmem(count):
    return [pl.BlockSpec(memory_space=pltpu.VMEM)] * count


def smem():
    return [pl.BlockSpec(memory_space=pltpu.SMEM)]


params = pltpu.CompilerParams(vmem_limit_bytes=vmem_bytes)


def cost(flops, moved):
    return pl.CostEstimate(flops=flops, bytes_accessed=moved, transcendentals=0)


def shifted(x, axis, step):
    size = lax.axis_size(axis)
    return lax.ppermute(x, axis, [(i, (i + step) % size) for i in range(size)])


def from_diagonal(x):
    lons, lats = lax.axis_size("lon"), lax.axis_size("lat")
    pairs = [
        (i * lats + j, (i - 1) % lons * lats + (j - 1) % lats)
        for i in range(lons)
        for j in range(lats)
    ]
    return lax.ppermute(x, ("lon", "lat"), pairs)


def every_peer(x):
    return lax.all_to_all(x, ("lon", "dp"), 0, 0, tiled=True)


def by_cell(x):
    return x[0].transpose(1, 2, 0, 3)


def local(
    output_first,
    output_second,
    cotangent_first,
    cotangent_second,
    norm_gain,
    w_qkv,
    w_proj,
    earth_bias,
    shifts,
    region,
):
    second_cells = by_cell(output_second)
    pair = jnp.concatenate((second_cells, by_cell(cotangent_first)), axis=-1)
    left, right = pair[:, 0:HALF], pair[:, HALF:WC]
    east = shifted(left, "lon", -1)
    diag = from_diagonal(left)
    south = shifted(right, "lat", -1)

    w_qkv_t = w_qkv.T

    bias, gain = pl.pallas_call(
        table_kernel,
        out_shape=(
            jax.ShapeDtypeStruct((2 * HEADS, ROWS, LANES), f32),
            jax.ShapeDtypeStruct((1, C), f32),
        ),
        in_specs=smem() + vmem(2),
        out_specs=tuple(vmem(2)),
        scratch_shapes=[
            pltpu.VMEM((16, WIDE), f32),
            pltpu.VMEM((GROUPS * PITCH, LANES), f32),
            pltpu.VMEM((2, 2 * HEADS, GROUPS, LANES), f32),
            pltpu.VMEM((GROUPS, LANES), f32),
        ],
        compiler_params=params,
        cost_estimate=cost(400_000_000, 2_000_000),
        name="bias_table",
    )(shifts, earth_bias.reshape(2 * HEADS, 1, POS), norm_gain.reshape(1, C))

    piece = functools.partial(jax.ShapeDtypeStruct, dtype=bf16)
    table_chunks = (CHUNKS, DEEP, 2, 128)
    own, to_south, bias_part = pl.pallas_call(
        attention_kernel,
        out_shape=(
            piece((WL, WC, LEVELS, 2 * C)),
            piece((WL - 1, WC, LEVELS, 2 * C)),
            piece(table_chunks),
        ),
        in_specs=smem() + vmem(9),
        out_specs=tuple(vmem(3)),
        scratch_shapes=[
            pltpu.VMEM((CELLS, 2 * C), f32),
            pltpu.VMEM((2, ROWS, C), bf16),
            pltpu.VMEM((2, ROWS, C), bf16),
            pltpu.VMEM((2, C, ROWS), bf16),
            pltpu.VMEM((2, C, ROWS), bf16),
            pltpu.VMEM((2, C, LANES), bf16),
            pltpu.VMEM((2, C, LANES), bf16),
            pltpu.VMEM((2, HEADS, ROWS, LANES), bf16),
            pltpu.VMEM((2, HEADS, ROWS, LANES), bf16),
            pltpu.VMEM((2, C, ROWS), bf16),
            pltpu.VMEM((2, C, ROWS), bf16),
            pltpu.VMEM((2, C, LANES), bf16),
            pltpu.VMEM((2, C, LANES), bf16),
            pltpu.VMEM((2, 16, 16, LANES), f32),
            pltpu.VMEM((16, WIDE), f32),
            pltpu.VMEM(table_chunks, f32),
        ],
        compiler_params=params,
        cost_estimate=cost(4_000_000_000, 2_000_000),
        name="window_attention",
    )(shifts, right, east, south, diag, gain, w_qkv, w_qkv_t, w_proj, bias)
    north = shifted(to_south, "lat", 1)

    half_block = (WL, HALF, LEVELS, 2 * C)
    near, to_east = pl.pallas_call(
        unframe_kernel,
        out_shape=(piece(half_block), piece(half_block)),
        in_specs=smem() + vmem(2),
        out_specs=tuple(vmem(2)),
        compiler_params=params,
        cost_estimate=cost(20_000_000_000, 500_000),
        name="home_rows",
    )(shifts, own, north)
    west = shifted(to_east, "lon", 1)

    sums = pl.pallas_call(
        table_sum_kernel,
        out_shape=piece(table_chunks),
        in_specs=vmem(1) + [pl.BlockSpec(memory_space=pl.ANY)],
        out_specs=vmem(1)[0],
        compiler_params=params,
        cost_estimate=cost(100_000, 400_000),
        name="table_sum",
    )(every_peer(bias_part), near)
    bias_grad = pl.pallas_call(
        table_home_kernel,
        out_shape=jax.ShapeDtypeStruct((2 * HEADS, 1, POS), f32),
        in_specs=vmem(1),
        out_specs=vmem(1)[0],
        compiler_params=params,
        cost_estimate=cost(100_000, 400_000),
        name="table_home",
    )(every_peer(sums))

    block = jax.ShapeDtypeStruct((WL, WC, LEVELS, C), bf16)
    input_first, grad_second = pl.pallas_call(
        home_kernel,
        out_shape=(block, block),
        in_specs=vmem(7),
        out_specs=tuple(vmem(2)),
        scratch_shapes=[pltpu.VMEM((CELLS, 2 * C), f32)],
        compiler_params=params,
        cost_estimate=cost(20_000_000_000, 2_000_000),
        name="home",
    )(
        west,
        near,
        by_cell(output_first),
        second_cells,
        by_cell(cotangent_second),
        gain,
        w_proj,
    )
    return (
        input_first.transpose(2, 0, 1, 3)[None],
        grad_second.transpose(2, 0, 1, 3)[None],
        bias_grad.reshape(2, 1, HEADS, POS),
    )


def solution(mesh):
    block = P("dp", None, "lat", "lon", None)
    table = P(None, "lat", None, None)
    return jax.shard_map(
        local,
        mesh=mesh,
        in_specs=(block, block, block, block, P(), P(), P(), table, P(), P()),
        out_specs=(block, block, table),
        check_vma=False,
    )
```

```python
import functools

import jax
import jax.numpy as jnp
from jax import lax
from jax.experimental import pallas as pl
from jax.experimental.pallas import tpu as pltpu
from jax.sharding import PartitionSpec as P

C = 192
HEADS = 6
HEAD = 32
LEVELS = 4
WL = 6
WC = 12
HALF = 6
POS = 3312
CHUNK = 138
SPAN = 23
GROUPS = 12
ROWS = 144
LANES = 256
REACH = 384
CELLS = 288
PITCH = 16
WIDE = 3584
TILES = 156
CHUNKS = 32
DEEP = 5

norm_eps = 1e-05
mask_fill = -1e30
scale = HEAD**-0.5
vmem_bytes = 20 * 1024 * 1024

f32 = jnp.float32
bf16 = jnp.bfloat16


def iota(shape, dim):
    return lax.broadcasted_iota(jnp.int32, shape, dim)


def mm(a, b):
    return lax.dot_general(a, b, (((1,), (0,)), ((), ())), preferred_element_type=f32)


def mm_t(a, b):
    return lax.dot_general(a, b, (((1,), (1,)), ((), ())), preferred_element_type=f32)


def parts(index, size):
    return lax.div(index, jnp.int32(size)), lax.rem(index, jnp.int32(size))


def picks(index, count, dim):
    shape = (index.shape[0], count) if dim == 0 else (count, index.shape[1])
    return jnp.where(iota(shape, 1 - dim) == index, 1.0, 0.0).astype(bf16)


def line(size, dim):
    return iota((size, 1) if dim == 0 else (1, size), dim)


def query_cells(a, dim):
    column, group = parts(line(ROWS, dim), GROUPS)
    level, row = parts(group, WL)
    return (row * WC + column) * LEVELS + 2 * a + level


def key_cells(a, dim):
    group, column = parts(line(LANES, dim), PITCH)
    level, row = parts(group, WL)
    return jnp.where(
        (group < GROUPS) & (column < WC), (row * WC + column) * LEVELS + 2 * a + level, -1
    )


def spread_entries(level, part, dim):
    group, place = parts(line(LANES, dim), PITCH)
    group = group - level * WL - part
    count = SPAN - PITCH if part else PITCH
    return jnp.where(
        (group >= 0) & (group < WL) & (place < count),
        group * SPAN + place + part * PITCH,
        -1,
    )


def chunk_place(group, level):
    start = (((group // WL) * 2 + level) * WL + group % WL) * CHUNK
    return start // 128 * 128, start % 128


def table_kernel(
    shifts_ref,
    bias_ref,
    gain_ref,
    w_qkv_ref,
    expanded_out,
    gain_out,
    w_qkv_t_out,
    wide,
    pieces,
    tables,
    mask,
):
    gain_out[...] = gain_ref[...]
    same = picks(line(C, 0), C, 0)
    for part in range(3):
        block = w_qkv_ref[:, part * C : (part + 1) * C]
        w_qkv_t_out[part * C : (part + 1) * C, :] = mm_t(same, block).astype(bf16)
    wide[...] = jnp.zeros(wide.shape, f32)
    for a in range(2):
        for h in range(HEADS):
            wide[a * 8 + h : a * 8 + h + 1, 0:POS] = bias_ref[a * HEADS + h]
    totals = [jnp.zeros((GROUPS * PITCH, LANES), f32) for _ in range(2)]
    for level in range(2):
        for group in range(GROUPS):
            tile, shift = chunk_place(group, level)
            piece = wide[:, tile : tile + REACH]
            if shift:
                piece = pltpu.roll(piece, REACH - shift, 1)
            pieces[group * PITCH : (group + 1) * PITCH, :] = piece[:, 0:LANES]
        spreads = [picks(spread_entries(level, part, 1), LANES, 1) for part in range(2)]
        rest = pieces[...]
        for _ in range(3):
            top = rest.astype(bf16)
            for part in range(2):
                totals[part] = totals[part] + mm(top, spreads[part])
            rest = rest - top.astype(f32)
    for part in range(2):
        pieces[...] = totals[part]
        for group in range(GROUPS):
            for a in range(2):
                for h in range(HEADS):
                    row = group * PITCH + a * 8 + h
                    tables[part, a * HEADS + h, group : group + 1, :] = pieces[row : row + 1, :]

    first_row = lax.axis_index("lat") * WL
    edge = lax.axis_size("lat") * WL - shifts_ref[0] - first_row
    query_row = parts(line(GROUPS, 0), WL)[1]
    key_group, key_column = parts(line(LANES, 1), PITCH)
    key_row = parts(key_group, WL)[1]
    query_id = jnp.where(query_row >= edge, 1, 0)
    valid = (key_group < GROUPS) & (key_column < WC)
    key_id = jnp.where(valid, jnp.where(key_row >= edge, 1, 0), 2)
    mask[...] = jnp.where(query_id == key_id, 0.0, mask_fill)

    def expand(index, carry):
        first, second = tables[0, index], tables[1, index]
        for c in range(WC):
            shift = (c - WC + 1) % LANES
            bias = jnp.where(key_column >= WC - 1 - c, first, second)
            if shift:
                bias = pltpu.roll(bias, shift, 1)
            expanded_out[index, c * GROUPS : (c + 1) * GROUPS, :] = bias + mask[...]
        return carry

    lax.fori_loop(0, 2 * HEADS, expand, 0)


def unframe_kernel(shifts_ref, own_ref, other_ref, near_out, send_out):
    for r in range(WL):
        place = r - shifts_ref[0]

        @pl.when(place >= 0)
        def _():
            near_out[r] = own_ref[place, 0:HALF]
            send_out[r] = own_ref[place, HALF:WC]

        @pl.when(place < 0)
        def _():
            near_out[r] = other_ref[place + WL - 1, 0:HALF]
            send_out[r] = other_ref[place + WL - 1, HALF:WC]


def join_halves(left_ref, right_ref, joined):
    half = HALF * LEVELS
    for r in range(WL):
        start = 2 * r * half
        joined[start : start + half, :] = left_ref[r].astype(f32).reshape(half, 2 * C)
        joined[start + half : start + 2 * half, :] = (
            right_ref[r].astype(f32).reshape(half, 2 * C)
        )


def attention_kernel(
    shifts_ref,
    own_ref,
    east_ref,
    south_ref,
    diag_ref,
    gain_ref,
    w_qkv_t_ref,
    w_proj_ref,
    bias_ref,
    own_out,
    south_out,
    bias_out,
    framed,
    queries,
    ups,
    queries_t,
    ups_t,
    keys_t,
    values_t,
    weights_low,
    grads_low,
    attended_t,
    grad_query_t,
    grad_key_t,
    grad_value_t,
    table_grad,
    wide,
    packed_table,
):
    half = HALF * LEVELS
    for r in range(WL):
        place = r + shifts_ref[0]
        left = slice(2 * r * half, (2 * r + 1) * half)
        right = slice((2 * r + 1) * half, (2 * r + 2) * half)

        @pl.when(place < WL)
        def _():
            framed[left, :] = own_ref[place].astype(f32).reshape(half, 2 * C)
            framed[right, :] = east_ref[place].astype(f32).reshape(half, 2 * C)

        @pl.when(place >= WL)
        def _():
            framed[left, :] = south_ref[place - WL].astype(f32).reshape(half, 2 * C)
            framed[right, :] = diag_ref[place - WL].astype(f32).reshape(half, 2 * C)

    cells = framed[:, 0:C]
    cotangent = framed[:, C : 2 * C].astype(bf16)
    centered = cells - jnp.mean(cells, axis=-1, keepdims=True)
    inverse = lax.rsqrt(jnp.mean(centered * centered, axis=-1, keepdims=True) + norm_eps)
    hidden = (centered * inverse * gain_ref[...]).astype(bf16)

    w_proj = w_proj_ref[...]
    for a in range(2):
        to_queries = picks(query_cells(a, 0), CELLS, 0)
        turned = mm(to_queries, hidden).astype(bf16)
        turned_cot = mm(to_queries, cotangent).astype(bf16)
        spaced = mm(picks(key_cells(a, 0), CELLS, 0), hidden).astype(bf16)
        queries[a] = mm_t(turned, w_qkv_t_ref[0:C, :]).astype(bf16)
        queries_t[a] = mm_t(w_qkv_t_ref[0:C, :], turned).astype(bf16)
        keys_t[a] = mm_t(w_qkv_t_ref[C : 2 * C, :], spaced).astype(bf16)
        values_t[a] = mm_t(w_qkv_t_ref[2 * C : 3 * C, :], spaced).astype(bf16)
        ups[a] = mm_t(turned_cot, w_proj).astype(bf16)
        ups_t[a] = mm_t(w_proj, turned_cot).astype(bf16)

    table_grad[...] = jnp.zeros(table_grad.shape, f32)
    key_column = parts(line(LANES, 1), PITCH)[1]

    def one_head(h, carry):
        chosen = parts(line(C, 1), HEAD)[0] == h
        for a in range(2):
            query = jnp.where(chosen, queries[a], jnp.zeros((), bf16))
            up = jnp.where(chosen, ups[a], jnp.zeros((), bf16))
            scores = mm(query, keys_t[a]) * scale + bias_ref[a * HEADS + h]
            exponent = jnp.exp(scores - jnp.max(scores, axis=-1, keepdims=True))
            weights = exponent * (1.0 / jnp.sum(exponent, axis=-1, keepdims=True))
            grad_weights = mm(up, values_t[a])
            row_dot = jnp.sum(weights * grad_weights, axis=-1, keepdims=True)
            grad_scores = weights * (grad_weights - row_dot)
            weights_low[a, h] = weights.astype(bf16)
            grads_low[a, h] = grad_scores.astype(bf16)
            low = jnp.zeros((GROUPS, LANES), f32)
            high = jnp.zeros((GROUPS, LANES), f32)
            for c in range(WC):
                shift = WC - 1 - c
                turned_grad = grad_scores[c * GROUPS : (c + 1) * GROUPS]
                if shift:
                    turned_grad = pltpu.roll(turned_grad, shift, 1)
                kept = key_column >= shift
                low = low + jnp.where(kept, turned_grad, 0.0)
                high = high + jnp.where(kept, 0.0, turned_grad)
            table_grad[0, a * 8 + h, 0:GROUPS] = low
            table_grad[1, a * 8 + h, 0:GROUPS] = high
        return carry

    lax.fori_loop(0, HEADS, one_head, 0)

    group, place = parts(line(GROUPS * PITCH, 0), PITCH)
    to_groups = picks(place * PITCH + group, 256, 0)
    by_group = [
        mm(to_groups, table_grad[part].reshape(256, LANES).astype(bf16)).astype(bf16)
        for part in range(2)
    ]
    wide[...] = jnp.zeros(wide.shape, f32)
    for level in range(2):
        packed = sum(
            mm(by_group[part], picks(spread_entries(level, part, 0), REACH, 0))
            for part in range(2)
        )
        for group in range(GROUPS):
            tile, turn = chunk_place(group, level)
            piece = packed[group * PITCH : (group + 1) * PITCH]
            if turn:
                piece = pltpu.roll(piece, turn, 1)
            wide[:, tile : tile + REACH] += piece
    packed_table[...] = jnp.zeros(packed_table.shape, f32)
    for tile in range(TILES):
        chunk, slot, row, lanes = tile_place(tile)
        row = row // HEADS * 8 + row % HEADS
        packed_table[chunk, slot] = wide[row : row + 2, lanes]
    bias_out[...] = packed_table[...].astype(bf16)

    for h in range(HEADS):
        features = slice(h * HEAD, (h + 1) * HEAD)
        for a in range(2):
            weight, grad = weights_low[a, h], grads_low[a, h]
            attended_t[a, features, :] = mm_t(values_t[a, features, :], weight).astype(bf16)
            grad_value_t[a, features, :] = mm(ups_t[a, features, :], weight).astype(bf16)
            grad_query_t[a, features, :] = (
                mm_t(keys_t[a, features, :], grad) * scale
            ).astype(bf16)
            grad_key_t[a, features, :] = (
                mm(queries_t[a, features, :], grad) * scale
            ).astype(bf16)

    attended = jnp.zeros((CELLS, C), f32)
    coeffs = [jnp.zeros((CELLS, C), f32) for _ in range(3)]
    for a in range(2):
        from_queries = picks(query_cells(a, 1), CELLS, 1)
        from_keys = picks(key_cells(a, 1), CELLS, 1)
        attended = attended + mm_t(from_queries, attended_t[a])
        coeffs[0] = coeffs[0] + mm_t(from_queries, grad_query_t[a])
        coeffs[1] = coeffs[1] + mm_t(from_keys, grad_key_t[a])
        coeffs[2] = coeffs[2] + mm_t(from_keys, grad_value_t[a])
    framed[:, 0:C] = attended
    framed[:, C : 2 * C] = sum(
        mm(coeffs[part].astype(bf16), w_qkv_t_ref[part * C : (part + 1) * C, :])
        for part in range(3)
    )
    row_cells = WC * LEVELS
    for r in range(WL):
        row = framed[r * row_cells : (r + 1) * row_cells, :]
        row = row.reshape(WC, LEVELS, 2 * C).astype(bf16)
        own_out[r] = row
        if r:
            south_out[r - 1] = row


def home_kernel(
    west_ref,
    near_ref,
    output_first_ref,
    output_second_ref,
    cotangent_second_ref,
    gain_ref,
    w_proj_ref,
    input_first_out,
    grad_second_out,
    placed,
):
    join_halves(west_ref, near_ref, placed)
    shape = (WL, WC, LEVELS, C)
    mixed = mm(placed[:, 0:C].astype(bf16), w_proj_ref[...])
    first = output_first_ref[...].astype(f32).reshape(CELLS, C)
    input_first_out[...] = (first - mixed).reshape(shape).astype(bf16)

    cells = output_second_ref[...].astype(f32).reshape(CELLS, C)
    centered = cells - jnp.mean(cells, axis=-1, keepdims=True)
    inverse = lax.rsqrt(jnp.mean(centered * centered, axis=-1, keepdims=True) + norm_eps)
    normed = centered * inverse
    scaled = placed[:, C : 2 * C] * gain_ref[...]
    backward = inverse * (
        scaled
        - jnp.mean(scaled, axis=-1, keepdims=True)
        - normed * jnp.mean(scaled * normed, axis=-1, keepdims=True)
    )
    second = cotangent_second_ref[...].astype(f32).reshape(CELLS, C)
    grad_second_out[...] = (second + backward).reshape(shape).astype(bf16)


def tile_place(tile):
    chunk, slot = divmod(tile, DEEP)
    pair, column = divmod(tile, TILES // HEADS)
    return chunk, slot, 2 * pair, slice(column * 128, column * 128 + 128)


def table_sum_kernel(parts_ref, after_ref, sums_out):
    total = jnp.sum(parts_ref[...].astype(f32), axis=0).astype(bf16)
    for peer in range(CHUNKS):
        sums_out[peer] = total


def table_home_kernel(sums_ref, table_out):
    for tile in range(TILES):
        chunk, slot, row, lanes = tile_place(tile)
        sums = sums_ref[chunk, slot].astype(f32)
        width = min(128, POS - lanes.start)
        for place in range(2):
            table_out[row + place, :, lanes.start : lanes.start + width] = sums[
                place : place + 1, 0:width
            ]


def vmem(count):
    return [pl.BlockSpec(memory_space=pltpu.VMEM)] * count


def smem():
    return [pl.BlockSpec(memory_space=pltpu.SMEM)]


params = pltpu.CompilerParams(vmem_limit_bytes=vmem_bytes)


def cost(flops, moved):
    return pl.CostEstimate(flops=flops, bytes_accessed=moved, transcendentals=0)


def shifted(x, axis, step):
    size = lax.axis_size(axis)
    return lax.ppermute(x, axis, [(i, (i + step) % size) for i in range(size)])


def from_diagonal(x):
    lons, lats = lax.axis_size("lon"), lax.axis_size("lat")
    pairs = [
        (i * lats + j, (i - 1) % lons * lats + (j - 1) % lats)
        for i in range(lons)
        for j in range(lats)
    ]
    return lax.ppermute(x, ("lon", "lat"), pairs)


def every_peer(x):
    return lax.all_to_all(x, ("lon", "dp"), 0, 0, tiled=True)


def by_cell(x):
    return x[0].transpose(1, 2, 0, 3)


def local(
    output_first,
    output_second,
    cotangent_first,
    cotangent_second,
    norm_gain,
    w_qkv,
    w_proj,
    earth_bias,
    shifts,
    region,
):
    second_cells = by_cell(output_second)
    pair = jnp.concatenate((second_cells, by_cell(cotangent_first)), axis=-1)
    left, right = pair[:, 0:HALF], pair[:, HALF:WC]
    east = shifted(left, "lon", -1)
    diag = from_diagonal(left)
    south = shifted(right, "lat", -1)


    bias, gain, w_qkv_t = pl.pallas_call(
        table_kernel,
        out_shape=(
            jax.ShapeDtypeStruct((2 * HEADS, ROWS, LANES), f32),
            jax.ShapeDtypeStruct((1, C), f32),
            jax.ShapeDtypeStruct((3 * C, C), bf16),
        ),
        in_specs=smem() + vmem(3),
        out_specs=tuple(vmem(3)),
        scratch_shapes=[
            pltpu.VMEM((16, WIDE), f32),
            pltpu.VMEM((GROUPS * PITCH, LANES), f32),
            pltpu.VMEM((2, 2 * HEADS, GROUPS, LANES), f32),
            pltpu.VMEM((GROUPS, LANES), f32),
        ],
        compiler_params=params,
        cost_estimate=cost(400_000_000, 2_000_000),
        name="bias_table",
    )(shifts, earth_bias.reshape(2 * HEADS, 1, POS), norm_gain.reshape(1, C), w_qkv)

    piece = functools.partial(jax.ShapeDtypeStruct, dtype=bf16)
    table_chunks = (CHUNKS, DEEP, 2, 128)
    own, to_south, bias_part = pl.pallas_call(
        attention_kernel,
        out_shape=(
            piece((WL, WC, LEVELS, 2 * C)),
            piece((WL - 1, WC, LEVELS, 2 * C)),
            piece(table_chunks),
        ),
        in_specs=smem() + vmem(8),
        out_specs=tuple(vmem(3)),
        scratch_shapes=[
            pltpu.VMEM((CELLS, 2 * C), f32),
            pltpu.VMEM((2, ROWS, C), bf16),
            pltpu.VMEM((2, ROWS, C), bf16),
            pltpu.VMEM((2, C, ROWS), bf16),
            pltpu.VMEM((2, C, ROWS), bf16),
            pltpu.VMEM((2, C, LANES), bf16),
            pltpu.VMEM((2, C, LANES), bf16),
            pltpu.VMEM((2, HEADS, ROWS, LANES), bf16),
            pltpu.VMEM((2, HEADS, ROWS, LANES), bf16),
            pltpu.VMEM((2, C, ROWS), bf16),
            pltpu.VMEM((2, C, ROWS), bf16),
            pltpu.VMEM((2, C, LANES), bf16),
            pltpu.VMEM((2, C, LANES), bf16),
            pltpu.VMEM((2, 16, 16, LANES), f32),
            pltpu.VMEM((16, WIDE), f32),
            pltpu.VMEM(table_chunks, f32),
        ],
        compiler_params=params,
        cost_estimate=cost(4_000_000_000, 2_000_000),
        name="window_attention",
    )(shifts, right, east, south, diag, gain, w_qkv_t, w_proj, bias)
    north = shifted(to_south, "lat", 1)

    half_block = (WL, HALF, LEVELS, 2 * C)
    near, to_east = pl.pallas_call(
        unframe_kernel,
        out_shape=(piece(half_block), piece(half_block)),
        in_specs=smem() + vmem(2),
        out_specs=tuple(vmem(2)),
        compiler_params=params,
        cost_estimate=cost(20_000_000_000, 500_000),
        name="home_rows",
    )(shifts, own, north)
    west = shifted(to_east, "lon", 1)

    sums = pl.pallas_call(
        table_sum_kernel,
        out_shape=piece(table_chunks),
        in_specs=vmem(1) + [pl.BlockSpec(memory_space=pl.ANY)],
        out_specs=vmem(1)[0],
        compiler_params=params,
        cost_estimate=cost(100_000, 400_000),
        name="table_sum",
    )(every_peer(bias_part), near)
    bias_grad = pl.pallas_call(
        table_home_kernel,
        out_shape=jax.ShapeDtypeStruct((2 * HEADS, 1, POS), f32),
        in_specs=vmem(1),
        out_specs=vmem(1)[0],
        compiler_params=params,
        cost_estimate=cost(100_000, 400_000),
        name="table_home",
    )(every_peer(sums))

    block = jax.ShapeDtypeStruct((WL, WC, LEVELS, C), bf16)
    input_first, grad_second = pl.pallas_call(
        home_kernel,
        out_shape=(block, block),
        in_specs=vmem(7),
        out_specs=tuple(vmem(2)),
        scratch_shapes=[pltpu.VMEM((CELLS, 2 * C), f32)],
        compiler_params=params,
        cost_estimate=cost(20_000_000_000, 2_000_000),
        name="home",
    )(
        west,
        near,
        by_cell(output_first),
        second_cells,
        by_cell(cotangent_second),
        gain,
        w_proj,
    )
    return (
        input_first.transpose(2, 0, 1, 3)[None],
        grad_second.transpose(2, 0, 1, 3)[None],
        bias_grad.reshape(2, 1, HEADS, POS),
    )


def solution(mesh):
    block = P("dp", None, "lat", "lon", None)
    table = P(None, "lat", None, None)
    return jax.shard_map(
        local,
        mesh=mesh,
        in_specs=(block, block, block, block, P(), P(), P(), table, P(), P()),
        out_specs=(block, block, table),
        check_vma=False,
    )
```
